256 devices in a mesh: dp: 4 (over y_lo, core), row: 8 (over z), col: 8 (over y_hi, x).
Axes of the slice: x: 4, y: 4 (y_hi: 2, y_lo: 2; y = y_hi * 2 + y_lo), z: 8, core: 2. Of those that a mesh axis runs over, the one named last changes fastest.
Arguments:
- hidden: bfloat16 [4096, 28672], P(('dp', 'col'), 'row'), may hold values from -6 to 6
- codes: bfloat16 [28672, 4096], P('row', 'col'), may hold values from -1 to 1
- scales: float32 [224, 32], P('row', 'col'), may hold values from 0.004 to 0.016
- out_grad: bfloat16 [4096, 4096], P(('dp', 'row'), 'col'), may hold values from -6 to 6
Outputs:
- output: bfloat16 [4096, 4096], P(('dp', 'row'), 'col')
- input_grad: bfloat16 [4096, 28672], P(('dp', 'col'), 'row')
- weight_grad: float32 [28672, 4096], P(('row', 'dp'), 'col')
The draws below stay inside these ranges and needn't reach their ends.
All inputs are finite; a program needn't handle non-finite values.
Results may differ from the reference program's by a relative error of at most 0.0049.
Values may be sent and summed in bfloat16 or wider, within the bound.
A program may use at most 128 MiB of HBM per device.

```python
import math
import jax
import jax.numpy as jnp
from jax import lax

FF = 28672
D = 4096
BLOCK = 128
TOKENS = 4096


def steps_of(rng, shape, pieces, least, top_value):
    def one(position, blocks):
        draws = jax.random.uniform(jax.random.fold_in(jax.random.fold_in(rng, 6), position), (blocks,), jnp.float32, least / len(pieces), top_value / len(pieces))
        return jnp.repeat(jnp.exp(draws), shape[position] // blocks).reshape((-1,) + (1,) * (len(shape) - position - 1))

    gain = one(*pieces[0])
    for cut in pieces[1:]:
        gain = gain * one(*cut)
    return gain


def centred(key, shape, spread, most, shards=(), dtype=jnp.bfloat16):
    values = jax.random.normal(key, shape, jnp.float32) * spread
    if len(shards) > 0:
        values = steps_of(key, shape, shards, -0.22, 0.18) * values
    return jnp.clip(values, min=-most, max=most).astype(dtype)


def setup_inputs(seed: int = 0) -> dict:
    splits = jax.random.split(jax.random.key(seed), 5)
    return {
        "hidden": centred(splits[0], (TOKENS, FF), 1.0, 6.0, ((0, 32), (1, 8))),
        "codes": jnp.clip(jax.random.uniform(splits[1], (FF, D), jnp.float32, -1.0, 1.0) * steps_of(splits[1], (FF, D), ((0, 8), (1, 8)), -0.4, 0.0), -1.0, 1.0).astype(jnp.bfloat16),
        "scales": jnp.clip(jnp.exp(math.log(0.016) - 1.3862944 * jax.random.uniform(splits[2], (FF // BLOCK, D // BLOCK), jnp.float32) ** steps_of(splits[2], (FF // BLOCK, D // BLOCK), ((0, 8), (1, 8)), -0.2, 0.2)), 0.004, 0.016),
        "out_grad": centred(splits[3], (TOKENS, D), 1.0, 6.0, ((0, 32), (1, 8))),
    }


def dequantize(codes, scales):
    rows, cols = codes.shape
    blocks = codes.astype(jnp.float32).reshape(rows // BLOCK, BLOCK, cols // BLOCK, BLOCK)
    blocks = blocks * scales[:, None, :, None]
    return blocks.reshape(rows, cols).astype(jnp.bfloat16)

def reference(hidden, codes, scales, out_grad):
    weight = dequantize(codes, scales)
    output = jnp.dot(hidden, weight, preferred_element_type=jnp.float32).astype(jnp.bfloat16)
    input_grad = lax.dot_general(out_grad, weight, (((1,), (1,)), ((), ())), preferred_element_type=jnp.float32).astype(jnp.bfloat16)
    factor = 1.0 / math.sqrt(TOKENS)
    weight_grad = lax.dot_general(hidden, out_grad, (((0,), (0,)), ((), ())), preferred_element_type=jnp.float32) * factor
    return (output, input_grad, weight_grad)
```

```python
import functools
import math

import jax
import jax.numpy as jnp
from jax import lax
from jax.experimental import pallas as pl
from jax.experimental.pallas import tpu as pltpu
from jax.sharding import PartitionSpec as P

MESH = pl.DeviceIdType.MESH
F32, BF16 = jnp.float32, jnp.bfloat16
NX, NZ = 4, 8
HOPS = {("own", 1): 4, ("own", -1): 3, ("other", 1): 3, ("other", -1): 4}
COPIES = 96


def nt(a, b):
    return lax.dot_general(a, b, (((1,), (1,)), ((), ())), preferred_element_type=F32)


def nn(a, b):
    return lax.dot_general(a, b, (((1,), (0,)), ((), ())), preferred_element_type=F32)


def tn(a, b):
    return lax.dot_general(a, b, (((0,), (0,)), ((), ())), preferred_element_type=F32)


def kernel(
    factor,
    h_ref,
    codes_ref,
    scales_ref,
    g_ref,
    y_out,
    dh_out,
    dw_out,
    codes_own,
    codes_sent,
    w,
    w_sent,
    hg,
    gg,
    dhp,
    dh_r1,
    dh_s2,
    dh_r2,
    dh_sent,
    dh_o,
    yp,
    y_r,
    y_s,
    y_sent,
    y_got,
    y_o,
    dwp,
    dw_s0,
    dw_r0,
    dw_s1,
    dw_r1,
    dw_s2,
    dw_r2,
    dw_o,
    ssem,
    rsem,
    lsem,
):
    tok, quarter = 128, hg.shape[2]
    half = quarter // 2
    dp, z, col = lax.axis_index("dp"), lax.axis_index("row"), lax.axis_index("col")
    yl, c = dp // 2, lax.rem(dp, 2)
    yh, x = col // NX, lax.rem(col, NX)
    oyl, oyh, oc = 1 - yl, 1 - yh, 1 - c

    def dev(x=x, yh=yh, yl=yl, z=z, c=c):
        return {"dp": yl * 2 + c, "row": z, "col": yh * NX + x}

    def xat(o):
        return lax.rem(x + o + NX, NX)

    def zat(o):
        return lax.rem(z + o + 2 * NZ, NZ)

    xto = {1: dev(x=xat(1)), -1: dev(x=xat(-1))}
    zto = {1: dev(z=zat(1)), -1: dev(z=zat(-1))}
    y1, y2, y3 = dev(yl=oyl), dev(yh=oyh), dev(yl=oyl, yh=oyh)
    sib = dev(c=oc)

    def slot_rows(m, n=tok):
        return pl.multiple_of((lax.rem(m, 4) * 2 + m // 4) * tok, tok)

    def xrows(o):
        return pl.multiple_of(xat(o) * (2 * tok), 2 * tok)

    ids = {}
    sends = []

    def key(*k):
        if k not in ids:
            ids[k] = len(ids)
        return ids[k]

    def send(k, src, dst, to):
        i = key(*k)
        copy = pltpu.make_async_remote_copy(
            src_ref=src,
            dst_ref=dst,
            send_sem=ssem.at[i],
            recv_sem=rsem.at[i],
            device_id=to,
            device_id_type=MESH,
        )
        copy.start()
        sends.append(copy)

    def recv(k, dst):
        i = key(*k)
        pltpu.make_async_remote_copy(
            src_ref=dst,
            dst_ref=dst,
            send_sem=ssem.at[i],
            recv_sem=rsem.at[i],
            device_id=sib,
            device_id_type=MESH,
        ).wait_recv()

    local_ids = []

    def local(src, dst):
        i = len(local_ids)
        local_ids.append(i)
        copy = pltpu.make_async_copy(src, dst, lsem.at[i])
        copy.start()
        return copy

    barrier = pltpu.get_barrier_semaphore()
    everyone = [xto[1], xto[-1], zto[1], zto[-1], y1, y2, y3, sib, dev(yl=oyl, yh=oyh, c=oc)]
    for d in everyone:
        pl.semaphore_signal(barrier, inc=1, device_id=d, device_id_type=MESH)
    send_codes = []
    for j in range(2):
        rows = pl.multiple_of((2 * j + oyh) * quarter + c * half, half)
        send_codes.append(local(codes_ref.at[pl.ds(rows, half)], codes_sent.at[j]))
    own_codes = []
    for j in range(2):
        rows = pl.multiple_of((2 * j + yh) * quarter, quarter)
        own_codes.append(local(codes_ref.at[pl.ds(rows, quarter)], codes_own.at[j]))
    grows = slot_rows(z)
    hrows = pl.multiple_of((x * 2 + yh) * tok, tok)
    hrows2 = pl.multiple_of((x * 2 + oyh) * tok, tok)
    own_g = local(g_ref, gg.at[yh, pl.ds(grows, tok)])

    def hcols(j, h):
        return h_ref.at[:, pl.ds(pl.multiple_of((2 * j + h) * quarter, quarter), quarter)]

    own_h = [local(hcols(j, yh), hg.at[j, pl.ds(hrows, tok)]) for j in range(2)]
    pl.semaphore_wait(barrier, len(everyone))

    send(("g2",), g_ref, gg.at[yh, pl.ds(grows, tok)], y2)
    for way in (1, -1):
        send(("g", "own", way, 1), g_ref, gg.at[yh, pl.ds(grows, tok)], zto[way])
    for j in range(2):
        send(("h2", j), hcols(j, oyh), hg.at[j, pl.ds(hrows, tok)], y2)
    for j in range(2):
        for way in (1, -1):
            send(("h", "own", way, j), hcols(j, yh), hg.at[j, pl.ds(hrows, tok)], xto[way])

    unit = 64

    def dequantize(src, dst, q, first):
        def step(u, carry):
            rows = pl.ds(pl.multiple_of(u * unit, unit), unit)
            block = q * (quarter // 128) + (first + u) // 2
            for b in range(dst.shape[1] // 128):
                cols = pl.ds(b * 128, 128)
                tile = src[rows, cols].astype(F32) * scales_ref[block, b]
                dst[rows, cols] = tile.astype(BF16)
            return carry

        lax.fori_loop(0, dst.shape[0] // unit, step, 0)

    def gblock(who):
        return yh if who == "own" else oyh

    def g_hop(who, way, k):
        rows = slot_rows(zat(-k * way))
        place = gg.at[gblock(who), pl.ds(rows, tok)]
        recv(("g", who, way, k), place)
        if k < HOPS[who, way]:
            send(("g", who, way, k + 1), place, place, zto[way])

    for j in range(2):
        send_codes[j].wait()
        dequantize(codes_sent.at[j], w_sent.at[j], 2 * j + oyh, c * (half // unit))
    place = gg.at[oyh, pl.ds(grows, tok)]
    recv(("g2",), place)
    for way in (1, -1):
        send(("g", "other", way, 1), place, place, zto[way])
    for way in (1, -1):
        g_hop("own", way, 1)
    own_codes[0].wait()
    dequantize(codes_own.at[0], w.at[0, yh], yh, 0)
    for way in (1, -1):
        g_hop("other", way, 1)
    for way in (1, -1):
        g_hop("own", way, 2)
    own_codes[1].wait()
    dequantize(codes_own.at[1], w.at[1, yh], 2 + yh, 0)
    for j in range(2):
        place = hg.at[j, pl.ds(hrows2, tok)]
        recv(("h2", j), place)
        for way in (1, -1):
            send(("h", "other", way, j), place, place, xto[way])
    crows = pl.multiple_of(c * half, half)
    ocrows = pl.multiple_of(oc * half, half)
    for j in range(2):
        send(("w3", j), w_sent.at[j], w.at[j, yh, pl.ds(crows, half)], y3)

    def h_pass(who):
        h = gblock(who)
        for way in (1, -1):
            rows = pl.multiple_of((xat(-way) * 2 + h) * tok, tok)
            for j in (0, 1) if way == 1 else (1, 0):
                place = hg.at[j, pl.ds(rows, tok)]
                recv(("h", who, way, j), place)
                if j == (0 if way == 1 else 1):
                    send(("hh", who, way), place, place, xto[way])

    for way in (1, -1):
        g_hop("other", way, 2)
    h_pass("own")
    for k in (3, 4):
        for who in ("own", "other"):
            for way in (1, -1):
                if k <= HOPS[who, way]:
                    g_hop(who, way, k)
    own_g.wait()
    for cp in own_h:
        cp.wait()
    h_pass("other")

    def dest(e):
        return (oyh if e & 2 else yh), (oyl if e & 1 else yl)

    def dw_first(i, carry):
        j, d = i // 2, lax.rem(i, 2)
        total = None
        for o in (0, 1, 3):
            rows = pl.ds(xrows(o), 2 * tok)
            part = tn(hg[j, rows, :], gg[d, rows, :])
            total = part if total is None else total + part
        dwp[j, d] = total
        return carry

    lax.fori_loop(0, 4, dw_first, 0)

    for j in range(2):
        place = w.at[j, oyh, pl.ds(crows, half)]
        recv(("w3", j), place)
        send(("w1", j), place, place, sib)

    def h_last(who):
        h = gblock(who)
        rows = pl.multiple_of((xat(2) * 2 + h) * tok, tok)
        for way in (1, -1):
            recv(("hh", who, way), hg.at[0 if way == 1 else 1, pl.ds(rows, tok)])

    def dh_part(o, j):
        rows = pl.ds(xrows(o), 2 * tok)
        total = nt(gg[0, rows, :], w[j, 0]) + nt(gg[1, rows, :], w[j, 1])
        dhp[j, rows, :] = total.astype(BF16)

    order = ("other", "own")
    for j in range(2):
        recv(("w1", j), w.at[j, oyh, pl.ds(ocrows, half)])
        dh_part(2, j)
        way = 1 if j == 0 else -1
        for i, who in enumerate(order):
            rows = pl.multiple_of((xat(2) * 2 + gblock(who)) * tok, tok)
            send(("dh1", way, who), dhp.at[j, pl.ds(rows, tok)], dh_r1.at[j, i], xto[way])
    for way in (1, -1):
        j = 1 if way == 1 else 0
        dh_part(way, j)
        for i, who in enumerate(order):
            rows = pl.multiple_of((xat(way) * 2 + gblock(who)) * tok, tok)
            send(("dh2", way, who, j), dhp.at[j, pl.ds(rows, tok)], dh_r2.at[0 if way == 1 else 1, j, i], xto[way])

    for who in ("own", "other"):
        h_last(who)
    far = pl.ds(xrows(2), 2 * tok)
    for n, e in enumerate((1, 2, 3, 0)):
        d, j = dest(e)
        dwp[j, d] += tn(hg[j, far, :], gg[d, far, :])
        dw_s0[e] = dwp[j, d, pl.ds(ocrows, half), :].astype(BF16)
        send(("dw0", e), dw_s0.at[e], dw_r0.at[e], sib)

    def dw_sum(e):
        d, j = dest(e)
        recv(("dw0", e), dw_r0.at[e])
        return dwp[j, d, pl.ds(crows, half), :] + dw_r0[e].astype(F32)

    for e in (1, 2):
        dw_s1[e - 1] = dw_sum(e).astype(BF16)
        send(("dw1", e), dw_s1.at[e - 1], dw_r1.at[e - 1], y1)

    for way in (1, -1):
        dh_part(way, 0 if way == 1 else 1)

    def y_part(i, carry):
        d, o = i // NX, lax.rem(i, NX)
        rows = pl.ds(pl.multiple_of(o * (2 * tok), 2 * tok), 2 * tok)
        total = nn(hg[0, rows, :], w[0, d]) + nn(hg[1, rows, :], w[1, d])
        yp[d, rows, :] = total
        return carry

    lax.fori_loop(0, 2 * NX, y_part, 0)
    slots = {}
    for n, k in enumerate((who, way, hop) for (who, way), hops in HOPS.items() for hop in range(1, hops + 1)):
        slots[k] = n

    def y_own(who, o):
        return yp[gblock(who), pl.ds(slot_rows(zat(o)), tok), :]

    def y_hop(who, way, k):
        hops = HOPS[who, way]
        total = y_own(who, way * (hops - k + 1))
        if k > 1:
            before = slots[who, way, k - 1]
            recv(("y", who, way, k - 1), y_r.at[before])
            total = total + y_r[before].astype(F32)
        n = slots[who, way, k]
        y_s[n] = total.astype(BF16)
        send(("y", who, way, k), y_s.at[n], y_r.at[n], zto[way])

    rings = [("other", -1), ("own", 1), ("other", 1), ("own", -1)]
    for who, way in rings:
        y_hop(who, way, 1)

    for i, who in enumerate(order):
        for way in (1, -1):
            j = 0 if way == 1 else 1
            rows = pl.ds(pl.multiple_of((xat(way) * 2 + gblock(who)) * tok, tok), tok)
            recv(("dh1", way, who), dh_r1.at[j, i])
            dh_s2[j, i] = (dhp[j, rows, :].astype(F32) + dh_r1[j, i].astype(F32)).astype(BF16)
            send(("dh2", way, who, j), dh_s2.at[j, i], dh_r2.at[0 if way == 1 else 1, j, i], xto[way])
        for ring in rings:
            y_hop(*ring, 2 + i)
    for j in range(2):
        dh_part(0, j)

    recv(("dw1", 2), dw_r1.at[1])
    dw_s2[0] = ((dw_sum(3) + dw_r1[1].astype(F32)) * factor).astype(BF16)
    third = key("dw3", 0), key("dw3", 1)

    def third_copy(core, to):
        return pltpu.make_async_remote_copy(
            src_ref=dw_s2.at[0],
            dst_ref=dw_r2.at[core],
            send_sem=ssem.at[third[0]],
            recv_sem=rsem.at[third[0] + core],
            device_id=to,
            device_id_type=MESH,
        )

    last = third_copy(c, dev(yl=oyl, yh=oyh, c=yh))
    last.start()
    recv(("dw1", 1), dw_r1.at[0])
    mine = (dw_sum(0) + dw_r1[0].astype(F32)) * factor
    fourth = key("dw4")

    def fourth_copy(core):
        return pltpu.make_async_remote_copy(
            src_ref=dw_s2.at[1],
            dst_ref=dw_r2.at[core],
            send_sem=ssem.at[fourth],
            recv_sem=rsem.at[fourth],
            device_id=sib,
            device_id_type=MESH,
        )

    @pl.when(c == yh)
    def _():
        dw_o[pl.ds(crows, half), :] = mine

    @pl.when(c != yh)
    def _():
        dw_s2[1] = mine.astype(BF16)
        fourth_copy(c).start()

    for who, way in rings:
        if HOPS[who, way] == 4:
            y_hop(who, way, 4)

    def y_total(who):
        total = y_own(who, 0)
        for way in (1, -1):
            n = slots[who, way, HOPS[who, way]]
            recv(("y", who, way, HOPS[who, way]), y_r.at[n])
            total = total + y_r[n].astype(F32)
        return total

    y_sent[...] = y_total("other").astype(BF16)
    send(("y2",), y_sent, y_got, y2)

    outs = []
    total = y_total("own")
    recv(("y2",), y_got)
    y_o[...] = (total + y_got[...].astype(F32)).astype(BF16)
    outs.append(local(y_o, y_out))

    @pl.when(c == yh)
    def _():
        fourth_copy(oc).wait_recv()
        dw_o[pl.ds(ocrows, half), :] = dw_r2[oc].astype(F32)

    @pl.when(c != yh)
    def _():
        for core in range(2):
            third_copy(core, sib).wait_recv()
            dw_o[core * half : (core + 1) * half, :] = dw_r2[core].astype(F32)

    outs.append(local(dw_o, dw_out))

    for i, who in enumerate(order):
        for j in range(2):
            rows = pl.ds(pl.multiple_of((x * 2 + gblock(who)) * tok, tok), tok)
            total = dhp[j, rows, :].astype(F32)
            for n, way in enumerate((1, -1)):
                recv(("dh2", way, who, j), dh_r2.at[n, j, i])
                total = total + dh_r2[n, j, i].astype(F32)
            if who == "own":
                dh_o[2 * j + yh] = total.astype(BF16)
            else:
                dh_sent[j] = total.astype(BF16)
                send(("dh3", j), dh_sent.at[j], dh_o.at[2 * j + yh], y2)
    for j in range(2):
        for h, got in ((yh, False), (oyh, True)):
            q = 2 * j + h
            if got:
                recv(("dh3", j), dh_o.at[q])
            cols = pl.ds(pl.multiple_of(q * quarter, quarter), quarter)
            outs.append(local(dh_o.at[q], dh_out.at[:, cols]))

    for copy in outs:
        copy.wait()
    for copy in sends:
        copy.wait_send()
    last.wait_send()

    @pl.when(c != yh)
    def _():
        fourth_copy(c).wait_send()


def per_device(factor, hidden, codes, scales, out_grad):
    tok, rows = hidden.shape
    cols = codes.shape[1]
    quarter = rows // 4
    half = quarter // 2
    tokens = 8 * tok
    hbm = pl.BlockSpec(memory_space=pl.ANY)
    vmem = pltpu.VMEM
    macs = tokens * rows * cols
    return pl.pallas_call(
        functools.partial(kernel, factor),
        out_shape=(
            jax.ShapeDtypeStruct((tok, cols), BF16),
            jax.ShapeDtypeStruct((tok, rows), BF16),
            jax.ShapeDtypeStruct((quarter, cols), F32),
        ),
        in_specs=[hbm, hbm, pl.BlockSpec(memory_space=pltpu.SMEM), hbm],
        out_specs=(hbm, hbm, hbm),
        scratch_shapes=[
            vmem((2, quarter, cols), BF16),
            vmem((2, half, cols), BF16),
            vmem((2, 2, quarter, cols), BF16),
            vmem((2, half, cols), BF16),
            vmem((2, tokens, quarter), BF16),
            vmem((2, tokens, cols), BF16),
            vmem((2, tokens, quarter), BF16),
            vmem((2, 2, tok, quarter), BF16),
            vmem((2, 2, tok, quarter), BF16),
            vmem((2, 2, 2, tok, quarter), BF16),
            vmem((2, tok, quarter), BF16),
            vmem((4, tok, quarter), BF16),
            vmem((2, tokens, cols), F32),
            vmem((14, tok, cols), BF16),
            vmem((14, tok, cols), BF16),
            vmem((tok, cols), BF16),
            vmem((tok, cols), BF16),
            vmem((tok, cols), BF16),
            vmem((2, 2, quarter, cols), F32),
            vmem((4, half, cols), BF16),
            vmem((4, half, cols), BF16),
            vmem((2, half, cols), BF16),
            vmem((2, half, cols), BF16),
            vmem((2, half, cols), BF16),
            vmem((2, half, cols), BF16),
            vmem((quarter, cols), F32),
            pltpu.SemaphoreType.DMA((COPIES,)),
            pltpu.SemaphoreType.DMA((COPIES,)),
            pltpu.SemaphoreType.DMA((16,)),
        ],
        compiler_params=pltpu.CompilerParams(
            collective_id=0, has_side_effects=True, vmem_limit_bytes=58 * 1024 * 1024
        ),
        cost_estimate=pl.CostEstimate(
            flops=6 * macs, bytes_accessed=16 * tok * rows, transcendentals=0
        ),
    )(hidden, codes, scales, out_grad)


def solution(mesh):
    in_specs = (P(("dp", "col"), "row"), P("row", "col"), P("row", "col"), P(("dp", "row"), "col"))
    out_specs = (P(("dp", "row"), "col"), P(("dp", "col"), "row"), P(("row", "dp"), "col"))

    def step(hidden, codes, scales, out_grad):
        factor = 1.0 / math.sqrt(hidden.shape[0])
        return jax.shard_map(
            functools.partial(per_device, factor),
            mesh=mesh,
            in_specs=in_specs,
            out_specs=out_specs,
            check_vma=False,
        )(hidden, codes, scales, out_grad)

    return step
```

```python
import functools
import math

import jax
import jax.numpy as jnp
from jax import lax
from jax.experimental import pallas as pl
from jax.experimental.pallas import tpu as pltpu
from jax.sharding import PartitionSpec as P

MESH = pl.DeviceIdType.MESH
F32, BF16 = jnp.float32, jnp.bfloat16
NX, NZ = 4, 8
HOPS = {("own", 1): 4, ("own", -1): 3, ("other", 1): 3, ("other", -1): 4}
COPIES = 96


def nt(a, b):
    return lax.dot_general(a, b, (((1,), (1,)), ((), ())), preferred_element_type=F32)


def nn(a, b):
    return lax.dot_general(a, b, (((1,), (0,)), ((), ())), preferred_element_type=F32)


def tn(a, b):
    return lax.dot_general(a, b, (((0,), (0,)), ((), ())), preferred_element_type=F32)


def kernel(
    factor,
    h_ref,
    codes_ref,
    scales_hbm,
    g_ref,
    y_out,
    dh_out,
    dw_out,
    scales_ref,
    codes_own,
    codes_sent,
    w,
    w_sent,
    hg,
    gg,
    dhp,
    dh_r1,
    dh_s2,
    dh_r2,
    dh_sent,
    yp,
    y_r,
    y_s,
    y_sent,
    y_got,
    dwp,
    dw_s0,
    dw_r0,
    dw_s1,
    dw_r1,
    dw_s2,
    dw_r2,
    ssem,
    rsem,
    lsem,
):
    tok, quarter = h_ref.shape[0], hg.shape[2]
    half = quarter // 2
    dp, z, col = lax.axis_index("dp"), lax.axis_index("row"), lax.axis_index("col")
    yl, c = dp // 2, lax.rem(dp, 2)
    yh, x = col // NX, lax.rem(col, NX)
    oyl, oyh, oc = 1 - yl, 1 - yh, 1 - c

    def dev(x=x, yh=yh, yl=yl, z=z, c=c):
        return {"dp": yl * 2 + c, "row": z, "col": yh * NX + x}

    def xat(o):
        return lax.rem(x + o + NX, NX)

    def zat(o):
        return lax.rem(z + o + 2 * NZ, NZ)

    xto = {1: dev(x=xat(1)), -1: dev(x=xat(-1))}
    zto = {1: dev(z=zat(1)), -1: dev(z=zat(-1))}
    y1, y2, y3 = dev(yl=oyl), dev(yh=oyh), dev(yl=oyl, yh=oyh)
    sib = dev(c=oc)
    side = {"own": yh, "other": oyh}

    def slot_rows(m):
        return pl.multiple_of((lax.rem(m, 4) * 2 + m // 4) * tok, tok)

    def hslot(o, who):
        return pl.multiple_of((xat(o) * 2 + side[who]) * tok, tok)

    def pair(p):
        return pl.ds(pl.multiple_of(p * (2 * tok), 2 * tok), 2 * tok)

    def first(j, of=yl):
        return of if j == 0 else 1 - of

    ids, sends, outs, local_ids = {}, [], [], []

    def key(*k):
        return ids.setdefault(k, len(ids))

    def send(k, src, dst, to):
        i = key(*k)
        copy = pltpu.make_async_remote_copy(
            src_ref=src,
            dst_ref=dst,
            send_sem=ssem.at[i],
            recv_sem=rsem.at[i],
            device_id=to,
            device_id_type=MESH,
        )
        copy.start()
        sends.append(copy)

    def recv(k, dst):
        i = key(*k)
        pltpu.make_async_remote_copy(
            src_ref=dst,
            dst_ref=dst,
            send_sem=ssem.at[i],
            recv_sem=rsem.at[i],
            device_id=sib,
            device_id_type=MESH,
        ).wait_recv()

    def local(src, dst):
        i = len(local_ids)
        local_ids.append(i)
        copy = pltpu.make_async_copy(src, dst, lsem.at[i])
        copy.start()
        return copy

    barrier = pltpu.get_barrier_semaphore()
    everyone = [xto[1], xto[-1], zto[1], zto[-1], y1, y2, y3, sib, dev(yl=oyl, yh=oyh, c=oc)]
    for d in everyone:
        pl.semaphore_signal(barrier, inc=1, device_id=d, device_id_type=MESH)
    got_scales = local(scales_hbm, scales_ref)
    sent_quarter = [2 * j + oyh for j in range(2)]
    own_quarter = [2 * j + yh for j in range(2)]
    piece = quarter // 4

    def piece_rows(l, core):
        return pl.ds(pl.multiple_of((2 * l + core) * piece, piece), piece)

    crows = pl.multiple_of(c * half, half)
    ocrows = pl.multiple_of(oc * half, half)
    got_sent_codes = [
        local(
            codes_ref.at[pl.ds(pl.multiple_of(sent_quarter[j] * quarter + (2 * oyl + c) * piece, piece), piece)],
            codes_sent.at[j],
        )
        for j in range(2)
    ]
    got_codes = [
        local(codes_ref.at[pl.ds(pl.multiple_of(own_quarter[j] * quarter, quarter), quarter)], codes_own.at[j])
        for j in range(2)
    ]
    grows = pl.ds(slot_rows(z), tok)
    hrows = pl.ds(hslot(0, "own"), tok)
    hrows2 = pl.ds(hslot(0, "other"), tok)
    got_g = local(g_ref, gg.at[yh, grows])

    def cols_of(q):
        return pl.ds(pl.multiple_of(q * quarter, quarter), quarter)

    def hcols(j, h):
        return h_ref.at[:, cols_of(2 * first(j) + h)]

    got_h = [local(hcols(j, yh), hg.at[j, hrows]) for j in range(2)]
    pl.semaphore_wait(barrier, len(everyone))

    send(("g2",), g_ref, gg.at[yh, grows], y2)
    for way in (1, -1):
        send(("h", "own", way, 0), hcols(0, yh), hg.at[0, hrows], xto[way])
    for way in (1, -1):
        send(("g", "own", way, 1), g_ref, gg.at[yh, grows], zto[way])
    send(("h2", 0), hcols(0, oyh), hg.at[0, hrows], y2)
    for way in (1, -1):
        send(("h", "own", way, 1), hcols(1, yh), hg.at[1, hrows], xto[way])
    send(("h2", 1), hcols(1, oyh), hg.at[1, hrows], y2)

    unit = 32

    def dequantize(src, dst, q, start):
        def step(u, carry):
            rows = pl.ds(pl.multiple_of(u * unit, unit), unit)
            block = q * (quarter // 128) + (start + u) // (128 // unit)
            for b in range(dst.shape[1] // 128):
                cols = pl.ds(b * 128, 128)
                tile = src[rows, cols].astype(F32) * scales_ref[b, block]
                dst[rows, cols] = tile.astype(BF16)
            return carry

        lax.fori_loop(0, dst.shape[0] // unit, step, 0)

    def g_hop(who, way, k):
        place = gg.at[side[who], pl.ds(slot_rows(zat(-k * way)), tok)]
        recv(("g", who, way, k), place)
        if k < HOPS[who, way]:
            send(("g", who, way, k + 1), place, place, zto[way])

    def g_hops(who, k):
        for way in (1, -1):
            if k <= HOPS[who, way]:
                g_hop(who, way, k)

    def h_partner(j):
        place = hg.at[j, hrows2]
        for way in (1, -1):
            send(("h", "other", way, j), place, place, xto[way])

    small = tok // 2

    def h_pass(who, j):
        for way in (1, -1):
            row = hslot(-way, who)
            recv(("h", who, way, j), hg.at[j, pl.ds(row, tok)])
            place = hg.at[j, pl.ds(row + (0 if way == 1 else small), small)]
            send(("hh", who, way, j), place, place, xto[way])

    def h_last(who, j):
        row = hslot(2, who)
        for way in (1, -1):
            recv(("hh", who, way, j), hg.at[j, pl.ds(row + (0 if way == 1 else small), small)])

    got_scales.wait()
    for j in range(2):
        got_sent_codes[j].wait()
        dequantize(codes_sent.at[j], w_sent.at[j], sent_quarter[j], (2 * oyl + c) * (piece // unit))
        send(("w3", j), w_sent.at[j], w.at[j, yh, piece_rows(oyl, c)], y3)
    place = gg.at[oyh, grows]
    recv(("g2",), place)
    for way in (1, -1):
        send(("g", "other", way, 1), place, place, zto[way])
    g_hops("own", 1)
    got_codes[0].wait()
    dequantize(codes_own.at[0], w.at[0, yh], own_quarter[0], 0)
    g_hops("other", 1)
    h_pass("own", 0)
    g_hops("own", 2)
    recv(("h2", 0), hg.at[0, hrows2])
    h_partner(0)
    g_hops("other", 2)
    got_codes[1].wait()
    dequantize(codes_own.at[1], w.at[1, yh], own_quarter[1], 0)
    h_pass("own", 1)
    g_hops("own", 3)
    recv(("h2", 1), hg.at[1, hrows2])
    g_hops("other", 3)
    h_pass("other", 0)
    h_partner(1)

    def w_pass(j):
        place = w.at[j, oyh, piece_rows(yl, c)]
        recv(("w3", j), place)
        send(("wy", j), place, place, y1)
        send(("ws", j), place, place, sib)

    def w_relay(j):
        place = w.at[j, oyh, piece_rows(oyl, c)]
        recv(("wy", j), place)
        send(("wt", j), place, place, sib)

    def w_last(j):
        recv(("ws", j), w.at[j, oyh, piece_rows(yl, oc)])
        recv(("wt", j), w.at[j, oyh, piece_rows(oyl, oc)])

    w_pass(0)
    g_hops("own", 4)
    g_hops("other", 4)
    got_g.wait()
    for copy in got_h:
        copy.wait()
    h_last("own", 0)
    h_last("other", 0)

    def dw_part(e):
        j, d = e % 2, side["other" if e & 2 else "own"]
        dwp[j, d] = tn(hg[j], gg[d])
        dw_s0[e] = dwp[j, d, pl.ds(ocrows, half), :].astype(BF16)
        send(("dw0", e), dw_s0.at[e], dw_r0.at[e], sib)

    def dw_sum(e):
        j, d = e % 2, side["other" if e & 2 else "own"]
        recv(("dw0", e), dw_r0.at[e])
        return dwp[j, d, pl.ds(crows, half), :] + dw_r0[e].astype(F32)

    def dw_cross(e):
        dw_s1[e - 1] = dw_sum(e).astype(BF16)
        send(("dw1", e), dw_s1.at[e - 1], dw_r1.at[e - 1], y1)

    def dh_part(o, j):
        rows = pair(xat(o))
        total = nt(gg[0, rows, :], w[j, 0]) + nt(gg[1, rows, :], w[j, 1])
        dhp[j, rows, :] = total.astype(BF16)

    def added(way):
        return 0 if way == 1 else 1

    order = ("other", "own")

    def dh_far(who, way):
        j = added(way)
        send(("dh1", way, who), dhp.at[j, pl.ds(hslot(2, who), tok)], dh_r1.at[j, order.index(who)], xto[way])

    def dh_place(who, way, j):
        return dh_r2.at[0 if way == 1 else 1, j, order.index(who)]

    def dh_near(who, way):
        j = 1 - added(way)
        send(("dh2", way, who, j), dhp.at[j, pl.ds(hslot(way, who), tok)], dh_place(who, way, j), xto[way])

    def dh_add(who, way):
        i, j = order.index(who), added(way)
        recv(("dh1", way, who), dh_r1.at[j, i])
        own = dhp[j, pl.ds(hslot(way, who), tok), :].astype(F32)
        dh_s2[j, i] = (own + dh_r1[j, i].astype(F32)).astype(BF16)
        send(("dh2", way, who, j), dh_s2.at[j, i], dh_place(who, way, j), xto[way])

    def dh_total(who, js=(0, 1)):
        i = order.index(who)
        for j in js:
            total = dhp[j, pl.ds(hslot(0, who), tok), :].astype(F32)
            for n, way in enumerate((1, -1)):
                recv(("dh2", way, who, j), dh_r2.at[n, j, i])
                total = total + dh_r2[n, j, i].astype(F32)
            cols = cols_of(2 * j + yh)
            if who == "own":
                dh_out[:, cols] = total.astype(BF16)
            else:
                dh_sent[j] = total.astype(BF16)
                send(("dh3", j), dh_sent.at[j], dh_out.at[:, cols], y2)

    def y_part(o):
        rows = pair(lax.rem(z + o, NX))

        def step(d, carry):
            yp[d, rows, :] = nn(hg[0, rows, :], w[yl, d]) + nn(hg[1, rows, :], w[oyl, d])
            return carry

        lax.fori_loop(0, 2, step, 0)

    slots = {}
    for n, k in enumerate((who, way, hop) for (who, way), hops in HOPS.items() for hop in range(1, hops + 1)):
        slots[k] = n

    def y_own(who, o):
        return yp[side[who], pl.ds(slot_rows(zat(o)), tok), :]

    def y_hop(who, way, k):
        total = y_own(who, way * (HOPS[who, way] - k + 1))
        if k > 1:
            before = slots[who, way, k - 1]
            recv(("y", who, way, k - 1), y_r.at[before])
            total = total + y_r[before].astype(F32)
        n = slots[who, way, k]
        y_s[n] = total.astype(BF16)
        send(("y", who, way, k), y_s.at[n], y_r.at[n], zto[way])

    def y_hops(k, hops):
        for (who, way), n in HOPS.items():
            if n == hops:
                y_hop(who, way, k)

    third, fourth = key("dw3", 0), key("dw4")
    key("dw3", 1)

    def third_copy(core, to):
        return pltpu.make_async_remote_copy(
            src_ref=dw_s2.at[0],
            dst_ref=dw_r2.at[core],
            send_sem=ssem.at[third],
            recv_sem=rsem.at[third + core],
            device_id=to,
            device_id_type=MESH,
        )

    def fourth_copy(core):
        return pltpu.make_async_remote_copy(
            src_ref=dw_s2.at[1],
            dst_ref=dw_r2.at[core],
            send_sem=ssem.at[fourth],
            recv_sem=rsem.at[fourth],
            device_id=sib,
            device_id_type=MESH,
        )

    def y_total(who):
        total = y_own(who, 0)
        for way in (1, -1):
            n = slots[who, way, HOPS[who, way]]
            recv(("y", who, way, HOPS[who, way]), y_r.at[n])
            total = total + y_r[n].astype(F32)
        return total

    dw_part(2)
    w_pass(1)
    w_relay(0)
    dw_part(0)
    dw_cross(2)
    h_pass("other", 1)
    w_last(0)
    dh_part(2, 0)
    for who in order:
        dh_far(who, 1)
    dh_part(-1, 0)
    for who in order:
        dh_near(who, -1)
    w_relay(1)
    dh_part(1, 0)
    h_last("own", 1)
    h_last("other", 1)
    dw_part(3)
    dw_part(1)
    w_last(1)
    y_part(0)
    y_hops(1, 4)
    dh_part(2, 1)
    for who in order:
        dh_far(who, -1)
    dw_cross(1)
    y_part(3)
    y_hop("other", 1, 1)
    y_part(1)
    y_hop("own", -1, 1)
    y_hops(2, 4)
    recv(("dw1", 2), dw_r1.at[1])
    dw_s2[0] = ((dw_sum(3) + dw_r1[1].astype(F32)) * factor).astype(BF16)
    last = third_copy(c, dev(yl=oyl, yh=oyh, c=yh))
    last.start()
    dh_part(1, 1)
    dh_near("other", 1)
    dh_add("other", 1)
    dh_near("own", 1)
    y_part(2)
    y_hops(2, 3)
    dh_part(-1, 1)
    dh_add("own", 1)
    dh_part(0, 0)
    y_hops(3, 4)
    dh_add("other", -1)
    dh_part(0, 1)
    y_hops(3, 3)
    dh_total("other", (0,))
    dh_add("own", -1)
    y_hops(4, 4)
    recv(("dw1", 1), dw_r1.at[0])
    mine = (dw_sum(0) + dw_r1[0].astype(F32)) * factor

    @pl.when(c == yh)
    def _():
        dw_out[pl.ds(crows, half), :] = mine

    @pl.when(c != yh)
    def _():
        dw_s2[1] = mine.astype(BF16)
        fourth_copy(c).start()

    dh_total("other", (1,))

    @pl.when(c == yh)
    def _():
        fourth_copy(oc).wait_recv()
        dw_out[pl.ds(ocrows, half), :] = dw_r2[oc].astype(F32)

    @pl.when(c != yh)
    def _():
        for core in range(2):
            third_copy(core, sib).wait_recv()
            dw_out[core * half : (core + 1) * half, :] = dw_r2[core].astype(F32)

    y_sent[...] = y_total("other").astype(BF16)
    send(("y2",), y_sent, y_got, y2)
    total = y_total("own")
    recv(("y2",), y_got)
    y_out[...] = (total + y_got[...].astype(F32)).astype(BF16)
    dh_total("own")
    for j in range(2):
        recv(("dh3", j), dh_out.at[:, cols_of(2 * j + oyh)])
    for copy in sends:
        copy.wait_send()
    last.wait_send()

    @pl.when(c != yh)
    def _():
        fourth_copy(c).wait_send()


def per_device(factor, hidden, codes, scales, out_grad):
    tok, rows = hidden.shape
    scales = scales.T
    cols = codes.shape[1]
    quarter = rows // 4
    half = quarter // 2
    tokens = 8 * tok
    hbm = pl.BlockSpec(memory_space=pl.ANY)
    vmem = pltpu.VMEM
    macs = tokens * rows * cols
    return pl.pallas_call(
        functools.partial(kernel, factor),
        out_shape=(
            vmem((tok, cols), BF16),
            vmem((tok, rows), BF16),
            vmem((quarter, cols), F32),
        ),
        in_specs=[hbm] * 4,
        out_specs=(pl.BlockSpec(memory_space=vmem),) * 3,
        scratch_shapes=[
            pltpu.SMEM(scales.shape, F32),
            vmem((2, quarter, cols), BF16),
            vmem((2, quarter // 4, cols), BF16),
            vmem((2, 2, quarter, cols), BF16),
            vmem((2, quarter // 4, cols), BF16),
            vmem((2, tokens, quarter), BF16),
            vmem((2, tokens, cols), BF16),
            vmem((2, tokens, quarter), BF16),
            vmem((2, 2, tok, quarter), BF16),
            vmem((2, 2, tok, quarter), BF16),
            vmem((2, 2, 2, tok, quarter), BF16),
            vmem((2, tok, quarter), BF16),
            vmem((2, tokens, cols), F32),
            vmem((14, tok, cols), BF16),
            vmem((14, tok, cols), BF16),
            vmem((tok, cols), BF16),
            vmem((tok, cols), BF16),
            vmem((2, 2, quarter, cols), F32),
            vmem((4, half, cols), BF16),
            vmem((4, half, cols), BF16),
            vmem((2, half, cols), BF16),
            vmem((2, half, cols), BF16),
            vmem((2, half, cols), BF16),
            vmem((2, half, cols), BF16),
            pltpu.SemaphoreType.DMA((COPIES,)),
            pltpu.SemaphoreType.DMA((COPIES,)),
            pltpu.SemaphoreType.DMA((16,)),
        ],
        compiler_params=pltpu.CompilerParams(
            collective_id=0, has_side_effects=True, vmem_limit_bytes=52 * 1024 * 1024
        ),
        cost_estimate=pl.CostEstimate(
            flops=6 * macs, bytes_accessed=16 * tok * rows, transcendentals=0
        ),
    )(hidden, codes, scales, out_grad)


def solution(mesh):
    in_specs = (P(("dp", "col"), "row"), P("row", "col"), P("row", "col"), P(("dp", "row"), "col"))
    out_specs = (P(("dp", "row"), "col"), P(("dp", "col"), "row"), P(("row", "dp"), "col"))

    def step(hidden, codes, scales, out_grad):
        factor = 1.0 / math.sqrt(hidden.shape[0])
        return jax.shard_map(
            functools.partial(per_device, factor),
            mesh=mesh,
            in_specs=in_specs,
            out_specs=out_specs,
            check_vma=False,
        )(hidden, codes, scales, out_grad)

    return step
```

```python
import functools
import math

import jax
import jax.numpy as jnp
from jax import lax
from jax.experimental import pallas as pl
from jax.experimental.pallas import tpu as pltpu
from jax.sharding import PartitionSpec as P

MESH = pl.DeviceIdType.MESH
F32, BF16 = jnp.float32, jnp.bfloat16
NX, NZ = 4, 8
HOPS = {("own", 1): 4, ("own", -1): 3, ("other", 1): 3, ("other", -1): 4}
COPIES = 96


def nt(a, b):
    return lax.dot_general(a, b, (((1,), (1,)), ((), ())), preferred_element_type=F32)


def nn(a, b):
    return lax.dot_general(a, b, (((1,), (0,)), ((), ())), preferred_element_type=F32)


def tn(a, b):
    return lax.dot_general(a, b, (((0,), (0,)), ((), ())), preferred_element_type=F32)


def kernel(
    factor,
    h_ref,
    codes_ref,
    scales_hbm,
    g_ref,
    y_out,
    dh_out,
    dw_out,
    scales_ref,
    codes_own,
    codes_sent,
    w,
    w_sent,
    hg,
    gg,
    dhp,
    dh_r1,
    dh_s2,
    dh_r2,
    dh_sent,
    yp,
    y_r,
    y_s,
    y_sent,
    y_got,
    dwp,
    dw_s0,
    dw_r0,
    dw_s1,
    dw_r1,
    dw_s2,
    dw_r2,
    ssem,
    rsem,
    lsem,
):
    tok, quarter = h_ref.shape[0], hg.shape[2]
    half = quarter // 2
    dp, z, col = lax.axis_index("dp"), lax.axis_index("row"), lax.axis_index("col")
    yl, c = dp // 2, lax.rem(dp, 2)
    yh, x = col // NX, lax.rem(col, NX)
    oyl, oyh, oc = 1 - yl, 1 - yh, 1 - c

    def dev(x=x, yh=yh, yl=yl, z=z, c=c):
        return {"dp": yl * 2 + c, "row": z, "col": yh * NX + x}

    def xat(o):
        return lax.rem(x + o + NX, NX)

    def zat(o):
        return lax.rem(z + o + 2 * NZ, NZ)

    xto = {1: dev(x=xat(1)), -1: dev(x=xat(-1))}
    zto = {1: dev(z=zat(1)), -1: dev(z=zat(-1))}
    y1, y2, y3 = dev(yl=oyl), dev(yh=oyh), dev(yl=oyl, yh=oyh)
    sib = dev(c=oc)
    side = {"own": yh, "other": oyh}

    def slot_rows(m):
        return pl.multiple_of((lax.rem(m, 4) * 2 + m // 4) * tok, tok)

    def hslot(o, who):
        return pl.multiple_of((xat(o) * 2 + side[who]) * tok, tok)

    def pair(p):
        return pl.ds(pl.multiple_of(p * (2 * tok), 2 * tok), 2 * tok)

    def first(j, of=yl):
        return of if j == 0 else 1 - of

    ids, sends, outs, local_ids = {}, [], [], []

    def key(*k):
        return ids.setdefault(k, len(ids))

    def send(k, src, dst, to):
        i = key(*k)
        copy = pltpu.make_async_remote_copy(
            src_ref=src,
            dst_ref=dst,
            send_sem=ssem.at[i],
            recv_sem=rsem.at[i],
            device_id=to,
            device_id_type=MESH,
        )
        copy.start()
        sends.append(copy)

    def recv(k, dst):
        i = key(*k)
        pltpu.make_async_remote_copy(
            src_ref=dst,
            dst_ref=dst,
            send_sem=ssem.at[i],
            recv_sem=rsem.at[i],
            device_id=sib,
            device_id_type=MESH,
        ).wait_recv()

    def local(src, dst):
        i = len(local_ids)
        local_ids.append(i)
        copy = pltpu.make_async_copy(src, dst, lsem.at[i])
        copy.start()
        return copy

    barrier = pltpu.get_barrier_semaphore()
    everyone = [xto[1], xto[-1], zto[1], zto[-1], y1, y2, y3, sib, dev(yl=oyl, yh=oyh, c=oc)]
    for d in everyone:
        pl.semaphore_signal(barrier, inc=1, device_id=d, device_id_type=MESH)
    got_scales = local(scales_hbm, scales_ref)
    sent_quarter = [2 * j + oyh for j in range(2)]
    own_quarter = [2 * j + yh for j in range(2)]
    piece = quarter // 4

    def piece_rows(l, core):
        return pl.ds(pl.multiple_of((2 * l + core) * piece, piece), piece)

    crows = pl.multiple_of(c * half, half)
    ocrows = pl.multiple_of(oc * half, half)
    got_sent_codes = [
        local(
            codes_ref.at[pl.ds(pl.multiple_of(sent_quarter[j] * quarter + (2 * oyl + c) * piece, piece), piece)],
            codes_sent.at[j],
        )
        for j in range(2)
    ]
    got_codes = [
        local(codes_ref.at[pl.ds(pl.multiple_of(own_quarter[j] * quarter, quarter), quarter)], codes_own.at[j])
        for j in range(2)
    ]
    grows = pl.ds(slot_rows(z), tok)
    hrows = pl.ds(hslot(0, "own"), tok)
    hrows2 = pl.ds(hslot(0, "other"), tok)
    got_g = local(g_ref, gg.at[yh, grows])

    def cols_of(q):
        return pl.ds(pl.multiple_of(q * quarter, quarter), quarter)

    def hcols(j, h):
        return h_ref.at[:, cols_of(2 * first(j) + h)]

    got_h = [local(hcols(j, yh), hg.at[j, hrows]) for j in range(2)]
    pl.semaphore_wait(barrier, len(everyone))

    send(("g2",), g_ref, gg.at[yh, grows], y2)
    for way in (1, -1):
        send(("h", "own", way, 0), hcols(0, yh), hg.at[0, hrows], xto[way])
    for way in (1, -1):
        send(("g", "own", way, 1), g_ref, gg.at[yh, grows], zto[way])
    send(("h2", 0), hcols(0, oyh), hg.at[0, hrows], y2)
    for way in (1, -1):
        send(("h", "own", way, 1), hcols(1, yh), hg.at[1, hrows], xto[way])

    unit = 32

    def dequantize(src, dst, q, start):
        def step(u, carry):
            rows = pl.ds(pl.multiple_of(u * unit, unit), unit)
            block = q * (quarter // 128) + (start + u) // (128 // unit)
            for b in range(dst.shape[1] // 128):
                cols = pl.ds(b * 128, 128)
                tile = src[rows, cols].astype(F32) * scales_ref[b, block]
                dst[rows, cols] = tile.astype(BF16)
            return carry

        lax.fori_loop(0, dst.shape[0] // unit, step, 0)

    def g_hop(who, way, k):
        place = gg.at[side[who], pl.ds(slot_rows(zat(-k * way)), tok)]
        recv(("g", who, way, k), place)
        if k < HOPS[who, way]:
            send(("g", who, way, k + 1), place, place, zto[way])

    def g_hops(who, k):
        for way in (1, -1):
            if k <= HOPS[who, way]:
                g_hop(who, way, k)

    def h_partner(j):
        place = hg.at[j, hrows2]
        for way in (1, -1):
            send(("h", "other", way, j), place, place, xto[way])

    small = tok // 2

    def h_pass(who, j):
        for way in (1, -1):
            row = hslot(-way, who)
            recv(("h", who, way, j), hg.at[j, pl.ds(row, tok)])
            place = hg.at[j, pl.ds(row + (0 if way == 1 else small), small)]
            send(("hh", who, way, j), place, place, xto[way])

    def h_last(who, j):
        row = hslot(2, who)
        for way in (1, -1):
            recv(("hh", who, way, j), hg.at[j, pl.ds(row + (0 if way == 1 else small), small)])

    got_scales.wait()
    for j in range(2):
        got_sent_codes[j].wait()
        dequantize(codes_sent.at[j], w_sent.at[j], sent_quarter[j], (2 * oyl + c) * (piece // unit))
        send(("w3", j), w_sent.at[j], w.at[j, yh, piece_rows(oyl, c)], y3)
        if j == 0:
            send(("h2", 1), hcols(1, oyh), hg.at[1, hrows], y2)
    for j in range(2):
        got_codes[j].wait()
        dequantize(codes_own.at[j], w.at[j, yh], own_quarter[j], 0)
    place = gg.at[oyh, grows]
    recv(("g2",), place)
    for way in (1, -1):
        send(("g", "other", way, 1), place, place, zto[way])
    g_hops("own", 1)
    h_pass("own", 0)
    g_hops("other", 1)
    recv(("h2", 0), hg.at[0, hrows2])
    h_partner(0)
    g_hops("own", 2)
    h_pass("own", 1)
    g_hops("other", 2)
    def y_rows(who, rows):
        d = side[who]
        yp[d, rows, :] = nn(hg[0, rows, :], w[yl, d]) + nn(hg[1, rows, :], w[oyl, d])

    def y_part(o):
        y_rows("other", pair(lax.rem(z + o, NX)))

    def w_pass(j):
        place = w.at[j, oyh, piece_rows(yl, c)]
        recv(("w3", j), place)
        send(("wy", j), place, place, y1)
        send(("ws", j), place, place, sib)

    def w_relay(j):
        place = w.at[j, oyh, piece_rows(oyl, c)]
        recv(("wy", j), place)
        send(("wt", j), place, place, sib)

    def w_last(j):
        recv(("ws", j), w.at[j, oyh, piece_rows(yl, oc)])
        recv(("wt", j), w.at[j, oyh, piece_rows(oyl, oc)])

    def dw_part(e):
        j, d = e % 2, side["other" if e & 2 else "own"]
        dwp[j, d] = tn(hg[j], gg[d])
        dw_s0[e] = dwp[j, d, pl.ds(ocrows, half), :].astype(BF16)
        send(("dw0", e), dw_s0.at[e], dw_r0.at[e], sib)

    part = half // 2

    def dw_sum(e, start=0, size=half):
        j, d = e % 2, side["other" if e & 2 else "own"]
        own = dwp[j, d, pl.ds(pl.multiple_of(crows + start, part), size), :]
        return own + dw_r0[e, pl.ds(start, size), :].astype(F32)

    def dw_cross(e):
        recv(("dw0", e), dw_r0.at[e])
        for p in range(2):
            rows = pl.ds(p * part, part)
            dw_s1[e - 1, rows, :] = dw_sum(e, p * part, part).astype(BF16)
            send(("dw1", e, p), dw_s1.at[e - 1, rows], dw_r1.at[e - 1, rows], y1)

    def dh_part(o, j):
        rows = pair(xat(o))
        total = nt(gg[0, rows, :], w[j, 0]) + nt(gg[1, rows, :], w[j, 1])
        dhp[j, rows, :] = total.astype(BF16)

    def added(way):
        return 0 if way == 1 else 1

    order = ("other", "own")

    def dh_far(who, way):
        j = added(way)
        send(("dh1", way, who), dhp.at[j, pl.ds(hslot(2, who), tok)], dh_r1.at[j, order.index(who)], xto[way])

    def dh_place(who, way, j):
        return dh_r2.at[0 if way == 1 else 1, j, order.index(who)]

    def dh_near(who, way):
        j = 1 - added(way)
        send(("dh2", way, who, j), dhp.at[j, pl.ds(hslot(way, who), tok)], dh_place(who, way, j), xto[way])

    def dh_add(who, way):
        i, j = order.index(who), added(way)
        recv(("dh1", way, who), dh_r1.at[j, i])
        own = dhp[j, pl.ds(hslot(way, who), tok), :].astype(F32)
        dh_s2[j, i] = (own + dh_r1[j, i].astype(F32)).astype(BF16)
        send(("dh2", way, who, j), dh_s2.at[j, i], dh_place(who, way, j), xto[way])

    def dh_total(who, js=(0, 1)):
        i = order.index(who)
        for j in js:
            total = dhp[j, pl.ds(hslot(0, who), tok), :].astype(F32)
            for n, way in enumerate((1, -1)):
                recv(("dh2", way, who, j), dh_r2.at[n, j, i])
                total = total + dh_r2[n, j, i].astype(F32)
            cols = cols_of(2 * j + yh)
            if who == "own":
                dh_out[:, cols] = total.astype(BF16)
            else:
                dh_sent[j] = total.astype(BF16)
                send(("dh3", j), dh_sent.at[j], dh_out.at[:, cols], y2)

    slots = {}
    for n, k in enumerate((who, way, hop) for (who, way), hops in HOPS.items() for hop in range(1, hops + 1)):
        slots[k] = n

    def y_own(who, o):
        return yp[side[who], pl.ds(slot_rows(zat(o)), tok), :]

    def y_hop(who, way, k):
        total = y_own(who, way * (HOPS[who, way] - k + 1))
        if k > 1:
            before = slots[who, way, k - 1]
            recv(("y", who, way, k - 1), y_r.at[before])
            total = total + y_r[before].astype(F32)
        n = slots[who, way, k]
        y_s[n] = total.astype(BF16)
        send(("y", who, way, k), y_s.at[n], y_r.at[n], zto[way])

    fourth = key("dw4")
    third = [key("dw3", n) for n in range(4)][0]

    def third_copy(core, p, to):
        rows = pl.ds(p * part, part)
        return pltpu.make_async_remote_copy(
            src_ref=dw_s2.at[0, rows],
            dst_ref=dw_r2.at[core, rows],
            send_sem=ssem.at[third + p],
            recv_sem=rsem.at[third + 2 * p + core],
            device_id=to,
            device_id_type=MESH,
        )

    thirds = []

    def dw_third(p):
        rows = pl.ds(p * part, part)
        recv(("dw1", 2, p), dw_r1.at[1, rows])
        total = dw_sum(3, p * part, part) + dw_r1[1, rows, :].astype(F32)
        dw_s2[0, rows, :] = (total * factor).astype(BF16)
        copy = third_copy(c, p, dev(yl=oyl, yh=oyh, c=yh))
        copy.start()
        thirds.append(copy)

    def fourth_copy(core):
        return pltpu.make_async_remote_copy(
            src_ref=dw_s2.at[1],
            dst_ref=dw_r2.at[core],
            send_sem=ssem.at[fourth],
            recv_sem=rsem.at[fourth],
            device_id=sib,
            device_id_type=MESH,
        )

    def y_total(who):
        total = y_own(who, 0)
        for way in (1, -1):
            n = slots[who, way, HOPS[who, way]]
            recv(("y", who, way, HOPS[who, way]), y_r.at[n])
            total = total + y_r[n].astype(F32)
        return total

    w_pass(0)
    g_hops("own", 3)
    h_pass("other", 0)
    recv(("h2", 1), hg.at[1, hrows2])
    h_partner(1)
    got_g.wait()
    for copy in got_h:
        copy.wait()
    g_hops("other", 3)
    w_relay(0)
    g_hops("own", 4)
    g_hops("other", 4)
    w_pass(1)
    w_last(0)
    dh_part(2, 0)
    dh_part(-1, 0)
    h_last("own", 0)
    h_last("other", 0)
    h_pass("other", 1)
    for who in order:
        dh_far(who, 1)
    dh_near("other", -1)
    dw_part(2)
    y_rows("own", pair(x))
    dw_cross(2)
    for o in (1, -1):
        y_rows("own", pair(xat(o)))
    w_relay(1)
    dw_part(0)
    h_last("own", 1)
    h_last("other", 1)
    dw_part(3)
    y_rows("own", pair(xat(2)))
    y_hop("own", 1, 1)
    y_hop("own", -1, 1)
    w_last(1)
    dh_part(2, 1)
    dh_far("other", -1)
    dh_near("own", -1)
    dw_part(1)
    y_part(0)
    y_hop("other", -1, 1)
    dh_part(1, 1)
    dh_near("other", 1)
    y_part(3)
    y_hop("other", 1, 1)
    recv(("dw0", 3), dw_r0.at[3])
    dw_third(0)
    dw_cross(1)
    y_hop("own", 1, 2)
    y_hop("own", -1, 2)
    dh_part(1, 0)
    dh_add("other", 1)
    dh_near("own", 1)
    y_part(1)
    y_hop("other", -1, 2)
    dw_third(1)
    dh_part(-1, 1)
    dh_add("other", -1)
    dh_far("own", -1)
    y_part(2)
    y_hop("other", 1, 2)
    y_hop("own", 1, 3)
    y_hop("own", -1, 3)
    dh_add("own", 1)
    dh_part(0, 0)
    y_hop("other", -1, 3)
    y_hop("other", 1, 3)
    dh_part(0, 1)
    dh_total("other", (0,))
    y_hop("own", 1, 4)
    dh_total("other", (1,))
    y_hop("other", -1, 4)
    dh_add("own", -1)
    y_sent[...] = y_total("other").astype(BF16)
    send(("y2",), y_sent, y_got, y2)
    recv(("dw0", 0), dw_r0.at[0])
    for p in range(2):
        recv(("dw1", 1, p), dw_r1.at[0, pl.ds(p * part, part)])
    mine = (dw_sum(0) + dw_r1[0].astype(F32)) * factor

    @pl.when(c == yh)
    def _():
        dw_out[pl.ds(crows, half), :] = mine

    @pl.when(c != yh)
    def _():
        dw_s2[1] = mine.astype(BF16)
        fourth_copy(c).start()

    @pl.when(c == yh)
    def _():
        fourth_copy(oc).wait_recv()
        dw_out[pl.ds(ocrows, half), :] = dw_r2[oc].astype(F32)

    @pl.when(c != yh)
    def _():
        for core in range(2):
            for p in range(2):
                third_copy(core, p, sib).wait_recv()
            dw_out[core * half : (core + 1) * half, :] = dw_r2[core].astype(F32)

    total = y_total("own")
    recv(("y2",), y_got)
    y_out[...] = (total + y_got[...].astype(F32)).astype(BF16)
    dh_total("own")
    for j in range(2):
        recv(("dh3", j), dh_out.at[:, cols_of(2 * j + oyh)])
    for copy in sends:
        copy.wait_send()
    for copy in thirds:
        copy.wait_send()

    @pl.when(c != yh)
    def _():
        fourth_copy(c).wait_send()


def per_device(factor, hidden, codes, scales, out_grad):
    tok, rows = hidden.shape
    scales = scales.T
    cols = codes.shape[1]
    quarter = rows // 4
    half = quarter // 2
    tokens = 8 * tok
    hbm = pl.BlockSpec(memory_space=pl.ANY)
    vmem = pltpu.VMEM
    macs = tokens * rows * cols
    return pl.pallas_call(
        functools.partial(kernel, factor),
        out_shape=(
            vmem((tok, cols), BF16),
            vmem((tok, rows), BF16),
            vmem((quarter, cols), F32),
        ),
        in_specs=[hbm] * 4,
        out_specs=(pl.BlockSpec(memory_space=vmem),) * 3,
        scratch_shapes=[
            pltpu.SMEM(scales.shape, F32),
            vmem((2, quarter, cols), BF16),
            vmem((2, quarter // 4, cols), BF16),
            vmem((2, 2, quarter, cols), BF16),
            vmem((2, quarter // 4, cols), BF16),
            vmem((2, tokens, quarter), BF16),
            vmem((2, tokens, cols), BF16),
            vmem((2, tokens, quarter), BF16),
            vmem((2, 2, tok, quarter), BF16),
            vmem((2, 2, tok, quarter), BF16),
            vmem((2, 2, 2, tok, quarter), BF16),
            vmem((2, tok, quarter), BF16),
            vmem((2, tokens, cols), F32),
            vmem((14, tok, cols), BF16),
            vmem((14, tok, cols), BF16),
            vmem((tok, cols), BF16),
            vmem((tok, cols), BF16),
            vmem((2, 2, quarter, cols), F32),
            vmem((4, half, cols), BF16),
            vmem((4, half, cols), BF16),
            vmem((2, half, cols), BF16),
            vmem((2, half, cols), BF16),
            vmem((2, half, cols), BF16),
            vmem((2, half, cols), BF16),
            pltpu.SemaphoreType.DMA((COPIES,)),
            pltpu.SemaphoreType.DMA((COPIES,)),
            pltpu.SemaphoreType.DMA((16,)),
        ],
        compiler_params=pltpu.CompilerParams(
            collective_id=0, has_side_effects=True, vmem_limit_bytes=52 * 1024 * 1024
        ),
        cost_estimate=pl.CostEstimate(
            flops=6 * macs, bytes_accessed=16 * tok * rows, transcendentals=0
        ),
    )(hidden, codes, scales, out_grad)


def solution(mesh):
    in_specs = (P(("dp", "col"), "row"), P("row", "col"), P("row", "col"), P(("dp", "row"), "col"))
    out_specs = (P(("dp", "row"), "col"), P(("dp", "col"), "row"), P(("row", "dp"), "col"))

    def step(hidden, codes, scales, out_grad):
        factor = 1.0 / math.sqrt(hidden.shape[0])
        return jax.shard_map(
            functools.partial(per_device, factor),
            mesh=mesh,
            in_specs=in_specs,
            out_specs=out_specs,
            check_vma=False,
        )(hidden, codes, scales, out_grad)

    return step
```

```python
import functools
import math

import jax
import jax.numpy as jnp
from jax import lax
from jax.experimental import pallas as pl
from jax.experimental.pallas import tpu as pltpu
from jax.sharding import PartitionSpec as P

MESH = pl.DeviceIdType.MESH
F32, BF16 = jnp.float32, jnp.bfloat16
NX, NZ = 4, 8
HOPS = {("own", 1): 4, ("own", -1): 3, ("other", 1): 3, ("other", -1): 4}
COPIES = 96


def nt(a, b):
    return lax.dot_general(a, b, (((1,), (1,)), ((), ())), preferred_element_type=F32)


def nn(a, b):
    return lax.dot_general(a, b, (((1,), (0,)), ((), ())), preferred_element_type=F32)


def tn(a, b):
    return lax.dot_general(a, b, (((0,), (0,)), ((), ())), preferred_element_type=F32)


def kernel(
    factor,
    h_ref,
    codes_ref,
    scales_hbm,
    g_ref,
    y_out,
    dh_out,
    dw_out,
    scales_ref,
    codes_own,
    codes_sent,
    w,
    w_sent,
    hg,
    gg,
    dhp,
    dh_r1,
    dh_s2,
    dh_r2,
    dh_sent,
    yp,
    y_r,
    y_s,
    y_sent,
    y_got,
    dwp,
    dw_s0,
    dw_r0,
    dw_s1,
    dw_r1,
    dw_s2,
    dw_r2,
    ssem,
    rsem,
    lsem,
):
    tok, quarter = h_ref.shape[0], hg.shape[2]
    half = quarter // 2
    dp, z, col = lax.axis_index("dp"), lax.axis_index("row"), lax.axis_index("col")
    yl, c = dp // 2, lax.rem(dp, 2)
    yh, x = col // NX, lax.rem(col, NX)
    oyl, oyh, oc = 1 - yl, 1 - yh, 1 - c

    def dev(x=x, yh=yh, yl=yl, z=z, c=c):
        return {"dp": yl * 2 + c, "row": z, "col": yh * NX + x}

    def xat(o):
        return lax.rem(x + o + NX, NX)

    def zat(o):
        return lax.rem(z + o + 2 * NZ, NZ)

    xto = {1: dev(x=xat(1)), -1: dev(x=xat(-1))}
    zto = {1: dev(z=zat(1)), -1: dev(z=zat(-1))}
    y1, y2, y3 = dev(yl=oyl), dev(yh=oyh), dev(yl=oyl, yh=oyh)
    sib = dev(c=oc)
    side = {"own": yh, "other": oyh}

    def slot_rows(m):
        return pl.multiple_of((lax.rem(m, 4) * 2 + m // 4) * tok, tok)

    def hslot(o, who):
        return pl.multiple_of((xat(o) * 2 + side[who]) * tok, tok)

    def pair(p):
        return pl.ds(pl.multiple_of(p * (2 * tok), 2 * tok), 2 * tok)

    def first(j, of=yl):
        return of if j == 0 else 1 - of

    ids, sends, outs, local_ids = {}, [], [], []

    def key(*k):
        return ids.setdefault(k, len(ids))

    def send(k, src, dst, to):
        i = key(*k)
        copy = pltpu.make_async_remote_copy(
            src_ref=src,
            dst_ref=dst,
            send_sem=ssem.at[i],
            recv_sem=rsem.at[i],
            device_id=to,
            device_id_type=MESH,
        )
        copy.start()
        sends.append(copy)

    def recv(k, dst):
        i = key(*k)
        pltpu.make_async_remote_copy(
            src_ref=dst,
            dst_ref=dst,
            send_sem=ssem.at[i],
            recv_sem=rsem.at[i],
            device_id=sib,
            device_id_type=MESH,
        ).wait_recv()

    def local(src, dst):
        i = len(local_ids)
        local_ids.append(i)
        copy = pltpu.make_async_copy(src, dst, lsem.at[i])
        copy.start()
        return copy

    barrier = pltpu.get_barrier_semaphore()
    everyone = [xto[1], xto[-1], zto[1], zto[-1], y1, y2, y3, sib, dev(yl=oyl, yh=oyh, c=oc)]
    for d in everyone:
        pl.semaphore_signal(barrier, inc=1, device_id=d, device_id_type=MESH)
    got_scales = local(scales_hbm, scales_ref)
    sent_quarter = [2 * j + oyh for j in range(2)]
    own_quarter = [2 * j + yh for j in range(2)]
    piece = quarter // 4

    def piece_rows(l, core):
        return pl.ds(pl.multiple_of((2 * l + core) * piece, piece), piece)

    crows = pl.multiple_of(c * half, half)
    ocrows = pl.multiple_of(oc * half, half)
    got_sent_codes = [
        local(
            codes_ref.at[pl.ds(pl.multiple_of(sent_quarter[j] * quarter + (2 * oyl + c) * piece, piece), piece)],
            codes_sent.at[j],
        )
        for j in range(2)
    ]
    got_codes = [
        local(codes_ref.at[pl.ds(pl.multiple_of(own_quarter[j] * quarter, quarter), quarter)], codes_own.at[j])
        for j in range(2)
    ]
    grows = pl.ds(slot_rows(z), tok)
    hrows = pl.ds(hslot(0, "own"), tok)
    hrows2 = pl.ds(hslot(0, "other"), tok)
    got_g = local(g_ref, gg.at[yh, grows])

    def cols_of(q):
        return pl.ds(pl.multiple_of(q * quarter, quarter), quarter)

    def hcols(j, h):
        return h_ref.at[:, cols_of(2 * first(j) + h)]

    got_h = [local(hcols(j, yh), hg.at[j, hrows]) for j in range(2)]
    pl.semaphore_wait(barrier, len(everyone))

    send(("g2",), g_ref, gg.at[yh, grows], y2)
    for way in (1, -1):
        send(("h", "own", way, 0), hcols(0, yh), hg.at[0, hrows], xto[way])
    for way in (1, -1):
        send(("g", "own", way, 1), g_ref, gg.at[yh, grows], zto[way])
    send(("h2", 0), hcols(0, oyh), hg.at[0, hrows], y2)
    for way in (1, -1):
        send(("h", "own", way, 1), hcols(1, yh), hg.at[1, hrows], xto[way])

    unit = 32

    def dequantize(src, dst, q, start):
        def step(u, carry):
            rows = pl.ds(pl.multiple_of(u * unit, unit), unit)
            block = q * (quarter // 128) + (start + u) // (128 // unit)
            for b in range(dst.shape[1] // 128):
                cols = pl.ds(b * 128, 128)
                tile = src[rows, cols].astype(F32) * scales_ref[b, block]
                dst[rows, cols] = tile.astype(BF16)
            return carry

        lax.fori_loop(0, dst.shape[0] // unit, step, 0)

    def g_hop(who, way, k):
        place = gg.at[side[who], pl.ds(slot_rows(zat(-k * way)), tok)]
        recv(("g", who, way, k), place)
        if k < HOPS[who, way]:
            send(("g", who, way, k + 1), place, place, zto[way])

    def g_hops(who, k):
        for way in (1, -1):
            if k <= HOPS[who, way]:
                g_hop(who, way, k)

    def h_partner(j):
        place = hg.at[j, hrows2]
        for way in (1, -1):
            send(("h", "other", way, j), place, place, xto[way])

    small = tok // 2

    def h_pass(who, j):
        for way in (1, -1):
            row = hslot(-way, who)
            recv(("h", who, way, j), hg.at[j, pl.ds(row, tok)])
            place = hg.at[j, pl.ds(row + (0 if way == 1 else small), small)]
            send(("hh", who, way, j), place, place, xto[way])

    def h_last(who, j):
        row = hslot(2, who)
        for way in (1, -1):
            recv(("hh", who, way, j), hg.at[j, pl.ds(row + (0 if way == 1 else small), small)])

    got_scales.wait()
    for j in range(2):
        got_sent_codes[j].wait()
        dequantize(codes_sent.at[j], w_sent.at[j], sent_quarter[j], (2 * oyl + c) * (piece // unit))
        send(("w3", j), w_sent.at[j], w.at[j, yh, piece_rows(oyl, c)], y3)
        if j == 0:
            send(("h2", 1), hcols(1, oyh), hg.at[1, hrows], y2)
    for j in range(2):
        got_codes[j].wait()
        dequantize(codes_own.at[j], w.at[j, yh], own_quarter[j], 0)
    place = gg.at[oyh, grows]
    recv(("g2",), place)
    for way in (1, -1):
        send(("g", "other", way, 1), place, place, zto[way])
    g_hops("own", 1)
    h_pass("own", 0)
    g_hops("other", 1)
    recv(("h2", 0), hg.at[0, hrows2])
    h_partner(0)
    g_hops("own", 2)
    h_pass("own", 1)
    g_hops("other", 2)
    def y_rows(who, rows):
        d = side[who]
        yp[d, rows, :] = nn(hg[0, rows, :], w[yl, d]) + nn(hg[1, rows, :], w[oyl, d])

    def y_part(o):
        y_rows("other", pair(lax.rem(z + o, NX)))

    def w_pass(j):
        place = w.at[j, oyh, piece_rows(yl, c)]
        recv(("w3", j), place)
        send(("wy", j), place, place, y1)
        send(("ws", j), place, place, sib)

    def w_relay(j):
        place = w.at[j, oyh, piece_rows(oyl, c)]
        recv(("wy", j), place)
        send(("wt", j), place, place, sib)

    def w_last(j):
        recv(("ws", j), w.at[j, oyh, piece_rows(yl, oc)])
        recv(("wt", j), w.at[j, oyh, piece_rows(oyl, oc)])

    def dw_part(e):
        j, d = e % 2, side["other" if e & 2 else "own"]
        dwp[j, d] = tn(hg[j], gg[d])
        dw_s0[e] = dwp[j, d, pl.ds(ocrows, half), :].astype(BF16)
        send(("dw0", e), dw_s0.at[e], dw_r0.at[e], sib)

    part = half // 2

    def dw_sum(e, start=0, size=half):
        j, d = e % 2, side["other" if e & 2 else "own"]
        own = dwp[j, d, pl.ds(pl.multiple_of(crows + start, part), size), :]
        return own + dw_r0[e, pl.ds(start, size), :].astype(F32)

    def dw_cross(e):
        recv(("dw0", e), dw_r0.at[e])
        for p in range(2):
            rows = pl.ds(p * part, part)
            dw_s1[e - 1, rows, :] = dw_sum(e, p * part, part).astype(BF16)
            send(("dw1", e, p), dw_s1.at[e - 1, rows], dw_r1.at[e - 1, rows], y1)

    def dh_part(o, j):
        rows = pair(xat(o))
        total = nt(gg[0, rows, :], w[j, 0]) + nt(gg[1, rows, :], w[j, 1])
        dhp[j, rows, :] = total.astype(BF16)

    def added(way):
        return 0 if way == 1 else 1

    order = ("other", "own")

    def dh_far(who, way):
        j = added(way)
        send(("dh1", way, who), dhp.at[j, pl.ds(hslot(2, who), tok)], dh_r1.at[j, order.index(who)], xto[way])

    def dh_place(who, way, j):
        return dh_r2.at[0 if way == 1 else 1, j, order.index(who)]

    def dh_near(who, way):
        j = 1 - added(way)
        send(("dh2", way, who, j), dhp.at[j, pl.ds(hslot(way, who), tok)], dh_place(who, way, j), xto[way])

    def dh_add(who, way):
        i, j = order.index(who), added(way)
        recv(("dh1", way, who), dh_r1.at[j, i])
        own = dhp[j, pl.ds(hslot(way, who), tok), :].astype(F32)
        dh_s2[j, i] = (own + dh_r1[j, i].astype(F32)).astype(BF16)
        send(("dh2", way, who, j), dh_s2.at[j, i], dh_place(who, way, j), xto[way])

    def dh_total(who, js=(0, 1)):
        i = order.index(who)
        for j in js:
            total = dhp[j, pl.ds(hslot(0, who), tok), :].astype(F32)
            for n, way in enumerate((1, -1)):
                recv(("dh2", way, who, j), dh_r2.at[n, j, i])
                total = total + dh_r2[n, j, i].astype(F32)
            cols = cols_of(2 * j + yh)
            if who == "own":
                dh_out[:, cols] = total.astype(BF16)
            else:
                dh_sent[j] = total.astype(BF16)
                send(("dh3", j), dh_sent.at[j], dh_out.at[:, cols], y2)

    slots = {}
    for n, k in enumerate((who, way, hop) for (who, way), hops in HOPS.items() for hop in range(1, hops + 1)):
        slots[k] = n

    def y_own(who, o):
        return yp[side[who], pl.ds(slot_rows(zat(o)), tok), :]

    def y_hop(who, way, k):
        total = y_own(who, way * (HOPS[who, way] - k + 1))
        if k > 1:
            before = slots[who, way, k - 1]
            recv(("y", who, way, k - 1), y_r.at[before])
            total = total + y_r[before].astype(F32)
        n = slots[who, way, k]
        y_s[n] = total.astype(BF16)
        send(("y", who, way, k), y_s.at[n], y_r.at[n], zto[way])

    fourth = key("dw4")
    third = [key("dw3", n) for n in range(4)][0]

    def third_copy(core, p, to):
        rows = pl.ds(p * part, part)
        return pltpu.make_async_remote_copy(
            src_ref=dw_s2.at[0, rows],
            dst_ref=dw_r2.at[core, rows],
            send_sem=ssem.at[third + p],
            recv_sem=rsem.at[third + 2 * p + core],
            device_id=to,
            device_id_type=MESH,
        )

    thirds = []

    def dw_third(p):
        rows = pl.ds(p * part, part)
        recv(("dw1", 2, p), dw_r1.at[1, rows])
        total = dw_sum(3, p * part, part) + dw_r1[1, rows, :].astype(F32)
        dw_s2[0, rows, :] = (total * factor).astype(BF16)
        copy = third_copy(c, p, dev(yl=oyl, yh=oyh, c=yh))
        copy.start()
        thirds.append(copy)

    def fourth_copy(core):
        return pltpu.make_async_remote_copy(
            src_ref=dw_s2.at[1],
            dst_ref=dw_r2.at[core],
            send_sem=ssem.at[fourth],
            recv_sem=rsem.at[fourth],
            device_id=sib,
            device_id_type=MESH,
        )

    def y_total(who):
        total = y_own(who, 0)
        for way in (1, -1):
            n = slots[who, way, HOPS[who, way]]
            recv(("y", who, way, HOPS[who, way]), y_r.at[n])
            total = total + y_r[n].astype(F32)
        return total

    w_pass(0)
    g_hops("own", 3)
    h_pass("other", 0)
    recv(("h2", 1), hg.at[1, hrows2])
    h_partner(1)
    got_g.wait()
    for copy in got_h:
        copy.wait()
    g_hops("other", 3)
    w_relay(0)
    g_hops("own", 4)
    g_hops("other", 4)
    w_pass(1)
    w_last(0)
    dh_part(2, 0)
    dh_part(-1, 0)
    h_last("own", 0)
    h_last("other", 0)
    h_pass("other", 1)
    for who in order:
        dh_far(who, 1)
    dh_near("other", -1)
    dw_part(2)
    y_rows("own", pair(x))
    dw_cross(2)
    for o in (1, -1):
        y_rows("own", pair(xat(o)))
    w_relay(1)
    dw_part(0)
    h_last("own", 1)
    h_last("other", 1)
    dw_part(3)
    y_rows("own", pair(xat(2)))
    y_hop("own", 1, 1)
    y_hop("own", -1, 1)
    w_last(1)
    dh_part(2, 1)
    dh_far("other", -1)
    dh_near("own", -1)
    dw_part(1)
    y_part(0)
    y_hop("other", -1, 1)
    dh_part(1, 1)
    dh_near("other", 1)
    y_part(3)
    y_hop("other", 1, 1)
    recv(("dw0", 3), dw_r0.at[3])
    dw_third(0)
    dw_cross(1)
    y_hop("own", 1, 2)
    y_hop("own", -1, 2)
    dh_part(1, 0)
    dh_add("other", 1)
    dh_near("own", 1)
    y_part(1)
    y_hop("other", -1, 2)
    dw_third(1)
    dh_part(-1, 1)
    dh_add("other", -1)
    dh_far("own", -1)
    y_part(2)
    y_hop("other", 1, 2)
    y_hop("own", 1, 3)
    y_hop("own", -1, 3)
    dh_add("own", 1)
    dh_part(0, 0)
    dh_part(0, 1)
    y_hop("other", -1, 3)
    dh_total("other", (0,))
    y_hop("other", 1, 3)
    y_hop("own", 1, 4)
    dh_total("other", (1,))
    y_hop("other", -1, 4)
    dh_add("own", -1)
    y_sent[...] = y_total("other").astype(BF16)
    send(("y2",), y_sent, y_got, y2)
    recv(("dw0", 0), dw_r0.at[0])
    for p in range(2):
        recv(("dw1", 1, p), dw_r1.at[0, pl.ds(p * part, part)])
    mine = (dw_sum(0) + dw_r1[0].astype(F32)) * factor

    @pl.when(c == yh)
    def _():
        dw_out[pl.ds(crows, half), :] = mine

    @pl.when(c != yh)
    def _():
        dw_s2[1] = mine.astype(BF16)
        fourth_copy(c).start()

    @pl.when(c == yh)
    def _():
        fourth_copy(oc).wait_recv()
        dw_out[pl.ds(ocrows, half), :] = dw_r2[oc].astype(F32)

    @pl.when(c != yh)
    def _():
        for core in range(2):
            for p in range(2):
                third_copy(core, p, sib).wait_recv()
            dw_out[core * half : (core + 1) * half, :] = dw_r2[core].astype(F32)

    total = y_total("own")
    recv(("y2",), y_got)
    y_out[...] = (total + y_got[...].astype(F32)).astype(BF16)
    dh_total("own")
    for j in range(2):
        recv(("dh3", j), dh_out.at[:, cols_of(2 * j + oyh)])
    for copy in sends:
        copy.wait_send()
    for copy in thirds:
        copy.wait_send()

    @pl.when(c != yh)
    def _():
        fourth_copy(c).wait_send()


def per_device(factor, hidden, codes, scales, out_grad):
    tok, rows = hidden.shape
    scales = scales.T
    cols = codes.shape[1]
    quarter = rows // 4
    half = quarter // 2
    tokens = 8 * tok
    hbm = pl.BlockSpec(memory_space=pl.ANY)
    vmem = pltpu.VMEM
    macs = tokens * rows * cols
    return pl.pallas_call(
        functools.partial(kernel, factor),
        out_shape=(
            vmem((tok, cols), BF16),
            vmem((tok, rows), BF16),
            vmem((quarter, cols), F32),
        ),
        in_specs=[hbm] * 4,
        out_specs=(pl.BlockSpec(memory_space=vmem),) * 3,
        scratch_shapes=[
            pltpu.SMEM(scales.shape, F32),
            vmem((2, quarter, cols), BF16),
            vmem((2, quarter // 4, cols), BF16),
            vmem((2, 2, quarter, cols), BF16),
            vmem((2, quarter // 4, cols), BF16),
            vmem((2, tokens, quarter), BF16),
            vmem((2, tokens, cols), BF16),
            vmem((2, tokens, quarter), BF16),
            vmem((2, 2, tok, quarter), BF16),
            vmem((2, 2, tok, quarter), BF16),
            vmem((2, 2, 2, tok, quarter), BF16),
            vmem((2, tok, quarter), BF16),
            vmem((2, tokens, cols), F32),
            vmem((14, tok, cols), BF16),
            vmem((14, tok, cols), BF16),
            vmem((tok, cols), BF16),
            vmem((tok, cols), BF16),
            vmem((2, 2, quarter, cols), F32),
            vmem((4, half, cols), BF16),
            vmem((4, half, cols), BF16),
            vmem((2, half, cols), BF16),
            vmem((2, half, cols), BF16),
            vmem((2, half, cols), BF16),
            vmem((2, half, cols), BF16),
            pltpu.SemaphoreType.DMA((COPIES,)),
            pltpu.SemaphoreType.DMA((COPIES,)),
            pltpu.SemaphoreType.DMA((16,)),
        ],
        compiler_params=pltpu.CompilerParams(
            collective_id=0, has_side_effects=True, vmem_limit_bytes=52 * 1024 * 1024
        ),
        cost_estimate=pl.CostEstimate(
            flops=6 * macs, bytes_accessed=16 * tok * rows, transcendentals=0
        ),
    )(hidden, codes, scales, out_grad)


def solution(mesh):
    in_specs = (P(("dp", "col"), "row"), P("row", "col"), P("row", "col"), P(("dp", "row"), "col"))
    out_specs = (P(("dp", "row"), "col"), P(("dp", "col"), "row"), P(("row", "dp"), "col"))

    def step(hidden, codes, scales, out_grad):
        factor = 1.0 / math.sqrt(hidden.shape[0])
        return jax.shard_map(
            functools.partial(per_device, factor),
            mesh=mesh,
            in_specs=in_specs,
            out_specs=out_specs,
            check_vma=False,
        )(hidden, codes, scales, out_grad)

    return step
```

```python
import functools
import math

import jax
import jax.numpy as jnp
from jax import lax
from jax.experimental import pallas as pl
from jax.experimental.pallas import tpu as pltpu
from jax.sharding import PartitionSpec as P

MESH = pl.DeviceIdType.MESH
F32, BF16 = jnp.float32, jnp.bfloat16
NX, NZ = 4, 8
HOPS = {("own", 1): 4, ("own", -1): 3, ("other", 1): 3, ("other", -1): 4}
COPIES = 96


def nt(a, b):
    return lax.dot_general(a, b, (((1,), (1,)), ((), ())), preferred_element_type=F32)


def nn(a, b):
    return lax.dot_general(a, b, (((1,), (0,)), ((), ())), preferred_element_type=F32)


def tn(a, b):
    return lax.dot_general(a, b, (((0,), (0,)), ((), ())), preferred_element_type=F32)


def kernel(
    factor,
    h_ref,
    codes_ref,
    scales_hbm,
    g_ref,
    y_out,
    dh_out,
    dw_out,
    scales_ref,
    codes_own,
    codes_sent,
    w,
    w_sent,
    hg,
    gg,
    dhp,
    dh_r1,
    dh_s2,
    dh_r2,
    dh_sent,
    yp,
    y_r,
    y_s,
    y_sent,
    y_got,
    dwp,
    dw_s0,
    dw_r0,
    dw_s1,
    dw_r1,
    dw_s2,
    dw_r2,
    ssem,
    rsem,
    lsem,
):
    tok, quarter = h_ref.shape[0], hg.shape[2]
    half = quarter // 2
    dp, z, col = lax.axis_index("dp"), lax.axis_index("row"), lax.axis_index("col")
    yl, c = dp // 2, lax.rem(dp, 2)
    yh, x = col // NX, lax.rem(col, NX)
    oyl, oyh, oc = 1 - yl, 1 - yh, 1 - c

    def dev(x=x, yh=yh, yl=yl, z=z, c=c):
        return {"dp": yl * 2 + c, "row": z, "col": yh * NX + x}

    def xat(o):
        return lax.rem(x + o + NX, NX)

    def zat(o):
        return lax.rem(z + o + 2 * NZ, NZ)

    xto = {1: dev(x=xat(1)), -1: dev(x=xat(-1))}
    zto = {1: dev(z=zat(1)), -1: dev(z=zat(-1))}
    y1, y2, y3 = dev(yl=oyl), dev(yh=oyh), dev(yl=oyl, yh=oyh)
    sib = dev(c=oc)
    side = {"own": yh, "other": oyh}

    def slot_rows(m):
        return pl.multiple_of((lax.rem(m, 4) * 2 + m // 4) * tok, tok)

    def hslot(o, who):
        return pl.multiple_of((xat(o) * 2 + side[who]) * tok, tok)

    def pair(p):
        return pl.ds(pl.multiple_of(p * (2 * tok), 2 * tok), 2 * tok)

    def first(j, of=yl):
        return of if j == 0 else 1 - of

    ids, sends, outs, local_ids = {}, [], [], []

    def key(*k):
        return ids.setdefault(k, len(ids))

    def send(k, src, dst, to):
        i = key(*k)
        copy = pltpu.make_async_remote_copy(
            src_ref=src,
            dst_ref=dst,
            send_sem=ssem.at[i],
            recv_sem=rsem.at[i],
            device_id=to,
            device_id_type=MESH,
        )
        copy.start()
        sends.append(copy)

    def recv(k, dst):
        i = key(*k)
        pltpu.make_async_remote_copy(
            src_ref=dst,
            dst_ref=dst,
            send_sem=ssem.at[i],
            recv_sem=rsem.at[i],
            device_id=sib,
            device_id_type=MESH,
        ).wait_recv()

    def local(src, dst):
        i = len(local_ids)
        local_ids.append(i)
        copy = pltpu.make_async_copy(src, dst, lsem.at[i])
        copy.start()
        return copy

    barrier = pltpu.get_barrier_semaphore()
    everyone = [xto[1], xto[-1], zto[1], zto[-1], y1, y2, y3, sib, dev(yl=oyl, yh=oyh, c=oc)]
    for d in everyone:
        pl.semaphore_signal(barrier, inc=1, device_id=d, device_id_type=MESH)
    got_scales = local(scales_hbm, scales_ref)
    sent_quarter = [2 * j + oyh for j in range(2)]
    own_quarter = [2 * j + yh for j in range(2)]
    piece = quarter // 4

    def piece_rows(l, core):
        return pl.ds(pl.multiple_of((2 * l + core) * piece, piece), piece)

    crows = pl.multiple_of(c * half, half)
    ocrows = pl.multiple_of(oc * half, half)
    got_sent_codes = [
        local(
            codes_ref.at[pl.ds(pl.multiple_of(sent_quarter[j] * quarter + (2 * oyl + c) * piece, piece), piece)],
            codes_sent.at[j],
        )
        for j in range(2)
    ]
    got_codes = [
        local(codes_ref.at[pl.ds(pl.multiple_of(own_quarter[j] * quarter, quarter), quarter)], codes_own.at[j])
        for j in range(2)
    ]
    grows = pl.ds(slot_rows(z), tok)
    hrows = pl.ds(hslot(0, "own"), tok)
    hrows2 = pl.ds(hslot(0, "other"), tok)
    got_g = local(g_ref, gg.at[yh, grows])

    def cols_of(q):
        return pl.ds(pl.multiple_of(q * quarter, quarter), quarter)

    def hcols(j, h):
        return h_ref.at[:, cols_of(2 * first(j) + h)]

    got_h = [local(hcols(j, yh), hg.at[j, hrows]) for j in range(2)]
    pl.semaphore_wait(barrier, len(everyone))

    send(("g2",), g_ref, gg.at[yh, grows], y2)
    for way in (1, -1):
        send(("h", "own", way, 0), hcols(0, yh), hg.at[0, hrows], xto[way])
    for way in (1, -1):
        send(("g", "own", way, 1), g_ref, gg.at[yh, grows], zto[way])
    send(("h2", 0), hcols(0, oyh), hg.at[0, hrows], y2)
    for way in (1, -1):
        send(("h", "own", way, 1), hcols(1, yh), hg.at[1, hrows], xto[way])

    unit = 32

    def dequantize(src, dst, q, start):
        def step(u, carry):
            rows = pl.ds(pl.multiple_of(u * unit, unit), unit)
            block = q * (quarter // 128) + (start + u) // (128 // unit)
            for b in range(dst.shape[1] // 128):
                cols = pl.ds(b * 128, 128)
                tile = src[rows, cols].astype(F32) * scales_ref[b, block]
                dst[rows, cols] = tile.astype(BF16)
            return carry

        lax.fori_loop(0, dst.shape[0] // unit, step, 0)

    def g_hop(who, way, k):
        place = gg.at[side[who], pl.ds(slot_rows(zat(-k * way)), tok)]
        recv(("g", who, way, k), place)
        if k < HOPS[who, way]:
            send(("g", who, way, k + 1), place, place, zto[way])

    def g_hops(who, k):
        for way in (1, -1):
            if k <= HOPS[who, way]:
                g_hop(who, way, k)

    def h_partner(j):
        place = hg.at[j, hrows2]
        for way in (1, -1):
            send(("h", "other", way, j), place, place, xto[way])

    small = tok // 2

    def h_pass(who, j):
        for way in (1, -1):
            row = hslot(-way, who)
            recv(("h", who, way, j), hg.at[j, pl.ds(row, tok)])
            place = hg.at[j, pl.ds(row + (0 if way == 1 else small), small)]
            send(("hh", who, way, j), place, place, xto[way])

    def h_last(who, j):
        row = hslot(2, who)
        for way in (1, -1):
            recv(("hh", who, way, j), hg.at[j, pl.ds(row + (0 if way == 1 else small), small)])

    got_scales.wait()
    for j in range(2):
        got_sent_codes[j].wait()
        dequantize(codes_sent.at[j], w_sent.at[j], sent_quarter[j], (2 * oyl + c) * (piece // unit))
        send(("w3", j), w_sent.at[j], w.at[j, yh, piece_rows(oyl, c)], y3)
        if j == 0:
            send(("h2", 1), hcols(1, oyh), hg.at[1, hrows], y2)
    for j in range(2):
        got_codes[j].wait()
        dequantize(codes_own.at[j], w.at[j, yh], own_quarter[j], 0)
    place = gg.at[oyh, grows]
    recv(("g2",), place)
    for way in (1, -1):
        send(("g", "other", way, 1), place, place, zto[way])
    g_hops("own", 1)
    h_pass("own", 0)
    g_hops("other", 1)
    recv(("h2", 0), hg.at[0, hrows2])
    h_partner(0)
    g_hops("own", 2)
    h_pass("own", 1)
    g_hops("other", 2)
    def y_rows(who, rows):
        d = side[who]
        yp[d, rows, :] = nn(hg[0, rows, :], w[yl, d]) + nn(hg[1, rows, :], w[oyl, d])

    def y_part(o):
        y_rows("other", pair(lax.rem(z + o, NX)))

    def w_pass(j):
        place = w.at[j, oyh, piece_rows(yl, c)]
        recv(("w3", j), place)
        send(("wy", j), place, place, y1)
        send(("ws", j), place, place, sib)

    def w_relay(j):
        place = w.at[j, oyh, piece_rows(oyl, c)]
        recv(("wy", j), place)
        send(("wt", j), place, place, sib)

    def w_last(j):
        recv(("ws", j), w.at[j, oyh, piece_rows(yl, oc)])
        recv(("wt", j), w.at[j, oyh, piece_rows(oyl, oc)])

    def dw_part(e):
        j, d = e % 2, side["other" if e & 2 else "own"]
        dwp[j, d] = tn(hg[j], gg[d])
        dw_s0[e] = dwp[j, d, pl.ds(ocrows, half), :].astype(BF16)
        send(("dw0", e), dw_s0.at[e], dw_r0.at[e], sib)

    part = half // 2

    def dw_sum(e, start=0, size=half):
        j, d = e % 2, side["other" if e & 2 else "own"]
        own = dwp[j, d, pl.ds(pl.multiple_of(crows + start, part), size), :]
        return own + dw_r0[e, pl.ds(start, size), :].astype(F32)

    def dw_cross(e):
        recv(("dw0", e), dw_r0.at[e])
        for p in range(2):
            rows = pl.ds(p * part, part)
            dw_s1[e - 1, rows, :] = dw_sum(e, p * part, part).astype(BF16)
            send(("dw1", e, p), dw_s1.at[e - 1, rows], dw_r1.at[e - 1, rows], y1)

    def dh_part(o, j):
        rows = pair(xat(o))
        total = nt(gg[0, rows, :], w[j, 0]) + nt(gg[1, rows, :], w[j, 1])
        dhp[j, rows, :] = total.astype(BF16)

    def added(way):
        return 0 if way == 1 else 1

    order = ("other", "own")

    def dh_far(who, way):
        j = added(way)
        send(("dh1", way, who), dhp.at[j, pl.ds(hslot(2, who), tok)], dh_r1.at[j, order.index(who)], xto[way])

    def dh_place(who, way, j):
        return dh_r2.at[0 if way == 1 else 1, j, order.index(who)]

    def dh_near(who, way):
        j = 1 - added(way)
        send(("dh2", way, who, j), dhp.at[j, pl.ds(hslot(way, who), tok)], dh_place(who, way, j), xto[way])

    def dh_add(who, way):
        i, j = order.index(who), added(way)
        recv(("dh1", way, who), dh_r1.at[j, i])
        own = dhp[j, pl.ds(hslot(way, who), tok), :].astype(F32)
        dh_s2[j, i] = (own + dh_r1[j, i].astype(F32)).astype(BF16)
        send(("dh2", way, who, j), dh_s2.at[j, i], dh_place(who, way, j), xto[way])

    def dh_total(who, js=(0, 1)):
        i = order.index(who)
        for j in js:
            total = dhp[j, pl.ds(hslot(0, who), tok), :].astype(F32)
            for n, way in enumerate((1, -1)):
                recv(("dh2", way, who, j), dh_r2.at[n, j, i])
                total = total + dh_r2[n, j, i].astype(F32)
            cols = cols_of(2 * j + yh)
            if who == "own":
                dh_out[:, cols] = total.astype(BF16)
            else:
                dh_sent[j] = total.astype(BF16)
                send(("dh3", j), dh_sent.at[j], dh_out.at[:, cols], y2)

    slots = {}
    for n, k in enumerate((who, way, hop) for (who, way), hops in HOPS.items() for hop in range(1, hops + 1)):
        slots[k] = n

    def y_own(who, o):
        return yp[side[who], pl.ds(slot_rows(zat(o)), tok), :]

    def y_hop(who, way, k):
        total = y_own(who, way * (HOPS[who, way] - k + 1))
        if k > 1:
            before = slots[who, way, k - 1]
            recv(("y", who, way, k - 1), y_r.at[before])
            total = total + y_r[before].astype(F32)
        n = slots[who, way, k]
        y_s[n] = total.astype(BF16)
        send(("y", who, way, k), y_s.at[n], y_r.at[n], zto[way])

    fourth = key("dw4")
    third = [key("dw3", n) for n in range(4)][0]

    def third_copy(core, p, to):
        rows = pl.ds(p * part, part)
        return pltpu.make_async_remote_copy(
            src_ref=dw_s2.at[0, rows],
            dst_ref=dw_r2.at[core, rows],
            send_sem=ssem.at[third + p],
            recv_sem=rsem.at[third + 2 * p + core],
            device_id=to,
            device_id_type=MESH,
        )

    thirds = []

    def dw_third(p):
        rows = pl.ds(p * part, part)
        recv(("dw1", 2, p), dw_r1.at[1, rows])
        total = dw_sum(3, p * part, part) + dw_r1[1, rows, :].astype(F32)
        dw_s2[0, rows, :] = (total * factor).astype(BF16)
        copy = third_copy(c, p, dev(yl=oyl, yh=oyh, c=yh))
        copy.start()
        thirds.append(copy)

    def fourth_copy(core):
        return pltpu.make_async_remote_copy(
            src_ref=dw_s2.at[1],
            dst_ref=dw_r2.at[core],
            send_sem=ssem.at[fourth],
            recv_sem=rsem.at[fourth],
            device_id=sib,
            device_id_type=MESH,
        )

    def y_total(who):
        total = y_own(who, 0)
        for way in (1, -1):
            n = slots[who, way, HOPS[who, way]]
            recv(("y", who, way, HOPS[who, way]), y_r.at[n])
            total = total + y_r[n].astype(F32)
        return total

    w_pass(0)
    g_hops("own", 3)
    h_pass("other", 0)
    recv(("h2", 1), hg.at[1, hrows2])
    h_partner(1)
    got_g.wait()
    for copy in got_h:
        copy.wait()
    g_hops("other", 3)
    w_relay(0)
    g_hops("own", 4)
    g_hops("other", 4)
    w_pass(1)
    w_last(0)
    dh_part(2, 0)
    dh_part(-1, 0)
    h_last("own", 0)
    h_last("other", 0)
    h_pass("other", 1)
    for who in order:
        dh_far(who, 1)
    dh_near("other", -1)
    dw_part(2)
    y_rows("own", pair(x))
    dw_cross(2)
    for o in (1, -1):
        y_rows("own", pair(xat(o)))
    w_relay(1)
    dw_part(0)
    h_last("own", 1)
    h_last("other", 1)
    dw_part(3)
    y_rows("own", pair(xat(2)))
    y_hop("own", 1, 1)
    y_hop("own", -1, 1)
    w_last(1)
    dh_part(2, 1)
    dh_far("other", -1)
    dh_near("own", -1)
    dw_part(1)
    y_part(0)
    y_hop("other", -1, 1)
    dh_part(1, 1)
    dh_near("other", 1)
    y_part(3)
    y_hop("other", 1, 1)
    dh_part(1, 0)
    dh_add("other", 1)
    dh_near("own", 1)
    recv(("dw0", 3), dw_r0.at[3])
    dw_third(0)
    dw_cross(1)
    y_hop("own", 1, 2)
    y_hop("own", -1, 2)
    y_part(1)
    y_hop("other", -1, 2)
    dw_third(1)
    dh_part(-1, 1)
    dh_add("other", -1)
    dh_far("own", -1)
    y_part(2)
    y_hop("other", 1, 2)
    y_hop("own", 1, 3)
    y_hop("own", -1, 3)
    dh_add("own", 1)
    dh_part(0, 0)
    dh_part(0, 1)
    y_hop("other", -1, 3)
    dh_total("other", (0,))
    y_hop("other", 1, 3)
    y_hop("own", 1, 4)
    dh_total("other", (1,))
    y_hop("other", -1, 4)
    dh_add("own", -1)
    y_sent[...] = y_total("other").astype(BF16)
    send(("y2",), y_sent, y_got, y2)
    recv(("dw0", 0), dw_r0.at[0])
    for p in range(2):
        recv(("dw1", 1, p), dw_r1.at[0, pl.ds(p * part, part)])
    mine = (dw_sum(0) + dw_r1[0].astype(F32)) * factor

    @pl.when(c == yh)
    def _():
        dw_out[pl.ds(crows, half), :] = mine

    @pl.when(c != yh)
    def _():
        dw_s2[1] = mine.astype(BF16)
        fourth_copy(c).start()

    @pl.when(c == yh)
    def _():
        fourth_copy(oc).wait_recv()
        dw_out[pl.ds(ocrows, half), :] = dw_r2[oc].astype(F32)

    @pl.when(c != yh)
    def _():
        for core in range(2):
            for p in range(2):
                third_copy(core, p, sib).wait_recv()
            dw_out[core * half : (core + 1) * half, :] = dw_r2[core].astype(F32)

    total = y_total("own")
    recv(("y2",), y_got)
    y_out[...] = (total + y_got[...].astype(F32)).astype(BF16)
    dh_total("own")
    for j in range(2):
        recv(("dh3", j), dh_out.at[:, cols_of(2 * j + oyh)])
    for copy in sends:
        copy.wait_send()
    for copy in thirds:
        copy.wait_send()

    @pl.when(c != yh)
    def _():
        fourth_copy(c).wait_send()


def per_device(factor, hidden, codes, scales, out_grad):
    tok, rows = hidden.shape
    scales = scales.T
    cols = codes.shape[1]
    quarter = rows // 4
    half = quarter // 2
    tokens = 8 * tok
    hbm = pl.BlockSpec(memory_space=pl.ANY)
    vmem = pltpu.VMEM
    macs = tokens * rows * cols
    return pl.pallas_call(
        functools.partial(kernel, factor),
        out_shape=(
            vmem((tok, cols), BF16),
            vmem((tok, rows), BF16),
            vmem((quarter, cols), F32),
        ),
        in_specs=[hbm] * 4,
        out_specs=(pl.BlockSpec(memory_space=vmem),) * 3,
        scratch_shapes=[
            pltpu.SMEM(scales.shape, F32),
            vmem((2, quarter, cols), BF16),
            vmem((2, quarter // 4, cols), BF16),
            vmem((2, 2, quarter, cols), BF16),
            vmem((2, quarter // 4, cols), BF16),
            vmem((2, tokens, quarter), BF16),
            vmem((2, tokens, cols), BF16),
            vmem((2, tokens, quarter), BF16),
            vmem((2, 2, tok, quarter), BF16),
            vmem((2, 2, tok, quarter), BF16),
            vmem((2, 2, 2, tok, quarter), BF16),
            vmem((2, tok, quarter), BF16),
            vmem((2, tokens, cols), F32),
            vmem((14, tok, cols), BF16),
            vmem((14, tok, cols), BF16),
            vmem((tok, cols), BF16),
            vmem((tok, cols), BF16),
            vmem((2, 2, quarter, cols), F32),
            vmem((4, half, cols), BF16),
            vmem((4, half, cols), BF16),
            vmem((2, half, cols), BF16),
            vmem((2, half, cols), BF16),
            vmem((2, half, cols), BF16),
            vmem((2, half, cols), BF16),
            pltpu.SemaphoreType.DMA((COPIES,)),
            pltpu.SemaphoreType.DMA((COPIES,)),
            pltpu.SemaphoreType.DMA((16,)),
        ],
        compiler_params=pltpu.CompilerParams(
            collective_id=0, has_side_effects=True, vmem_limit_bytes=52 * 1024 * 1024
        ),
        cost_estimate=pl.CostEstimate(
            flops=6 * macs, bytes_accessed=16 * tok * rows, transcendentals=0
        ),
    )(hidden, codes, scales, out_grad)


def solution(mesh):
    in_specs = (P(("dp", "col"), "row"), P("row", "col"), P("row", "col"), P(("dp", "row"), "col"))
    out_specs = (P(("dp", "row"), "col"), P(("dp", "col"), "row"), P(("row", "dp"), "col"))

    def step(hidden, codes, scales, out_grad):
        factor = 1.0 / math.sqrt(hidden.shape[0])
        return jax.shard_map(
            functools.partial(per_device, factor),
            mesh=mesh,
            in_specs=in_specs,
            out_specs=out_specs,
            check_vma=False,
        )(hidden, codes, scales, out_grad)

    return step
```
